256 devices in a mesh: tm: 32 (over z, x_lo, core), doc: 8 (over y, x_hi).
Axes of the slice: x: 4 (x_hi: 2, x_lo: 2; x = x_hi * 2 + x_lo), y: 4, z: 8, core: 2. Of those that a mesh axis runs over, the one named last changes fastest.
Arguments:
- beta: float32 [32, 16384, 128], P('tm', 'doc'), may hold values from -6 to 260
- word_ids: int32 [32, 32, 128], P('tm', 'doc'), may hold values from 0 to 16383
- word_counts: int32 [32, 32, 128], P('tm', 'doc'), may hold values from 1 to 8
- block_slot: int32 [128], replicated, may hold values from 0 to 127, each once
- topic_prior: float32 [128], replicated, may hold values from 0.05 to 0.5
- drift_var: float32 [128], replicated, may hold values from 0.0005 to 0.05
- obs_precision: float32 [32, 128], replicated, may hold values from 0.01 to 4
Outputs:
- smoothed_means: float32 [32, 16384, 128], P('tm', 'doc')
- doc_topics: float32 [32, 32, 128], P('tm', 'doc')
The draws below stay inside these ranges and needn't reach their ends.
Inputs may be any that keep to these rules, and one draw needn't show every extreme that they name: `block_slot`: each block has its own position.
All inputs are finite; a program needn't handle non-finite values.
Results may differ from the reference program's by a relative error of at most 0.0012.
The reference program's roundings to bfloat16 on the way (of `table`, `looked` and `weighted`) count: a program that leaves them out, or rounds other values in their place, can miss the bound.
Values may be sent and summed in bfloat16 or wider, within the bound.
A program may use at most 192 MiB of HBM per device.

```python
import math
import jax
import jax.numpy as jnp
import numpy as np
from jax import lax

K = 128
BLOCK = 128
TOK_DOC = 128
EITERS = 4
YEARS = 32
V = 16384
NBLOCKS = 128
DOCS = 32


def draw_beta(key, part):
    base_key = jax.random.fold_in(key, 0)
    return jnp.clip(1.5 * jax.random.normal(base_key, (YEARS, V, K), jnp.float32), -6.0, 6.0)


def plant(entries, rng, least, largest):
    longest = entries.shape.index(max(entries.shape))
    spots = []
    for shift in (0, 1):
        where = [jax.random.randint(jax.random.fold_in(rng, axis), (), 0, length) for axis, length in enumerate(entries.shape)]
        where[longest] = (where[longest] + shift) % entries.shape[longest]
        spots.append(tuple(where))
    return entries.at[spots[0]].set(least).at[spots[1]].set(largest)


def rank_bounds(count, slope):
    loads = [(1 << 20) // math.isqrt(standing ** slope) + 1 for standing in range(1, count + 1)]
    deviation = 1 + sum(loads) // (1 << 30)
    return np.cumsum(np.array([max(1, weight // deviation) for weight in loads]))


def ranked_ids(own_key, shape, amount, skew):
    grid = rank_bounds(amount, skew)
    lot = jax.random.randint(jax.random.fold_in(own_key, 1), shape, 0, int(grid[amount - 1]))
    grade = jnp.searchsorted(jnp.asarray(grid, jnp.int32), lot, side="right")
    return jax.random.permutation(jax.random.fold_in(own_key, 2), amount)[grade].astype(jnp.int32)


def setup_inputs(seed: int = 0) -> dict:
    splits = jax.random.split(jax.random.key(seed), 8)
    beta = draw_beta(jax.random.fold_in(splits[7], 71), 0)
    word_ids = plant(ranked_ids(splits[1], (YEARS, DOCS, TOK_DOC), V, 2), jax.random.fold_in(splits[1], 3), 0, V - 1).astype(jnp.int32)
    word_counts = plant(jax.random.randint(splits[2], (YEARS, DOCS, TOK_DOC), 1, 9), jax.random.fold_in(splits[2], 1), 1, 8).astype(jnp.int32)
    block_slot = jax.random.permutation(splits[3], NBLOCKS).astype(jnp.int32)
    topic_prior = jnp.clip(jnp.exp(jax.random.uniform(splits[4], (K,), jnp.float32, math.log(0.05), math.log(0.5))), 0.05, 0.5)
    drift_var = jnp.clip(jnp.exp(jax.random.uniform(splits[5], (K,), jnp.float32, math.log(0.0005), math.log(0.05))), 0.0005, 0.05)
    obs_precision = jnp.clip(jnp.exp(jax.random.uniform(splits[6], (YEARS, K), jnp.float32, math.log(0.01), math.log(4.0))), 0.01, 4.0)
    return dict(beta=beta, word_ids=word_ids, word_counts=word_counts, block_slot=block_slot, topic_prior=topic_prior, drift_var=drift_var, obs_precision=obs_precision)


init_variance = 4.0


def variance_tables(obs_precision, drift_var):
    def forward_step(prior_var, precision):
        denominator = 1.0 + prior_var * precision
        gain_now = prior_var * precision / denominator
        filt_var = prior_var / denominator
        return filt_var + drift_var, (gain_now, filt_var)

    start_var = jnp.full(drift_var.shape, init_variance, dtype=jnp.float32)
    last_var, (gains, filt_vars) = lax.scan(forward_step, start_var, obs_precision)

    def backward_step(info_next, precision):
        merged = info_next + precision
        shrink = 1.0 / (1.0 + drift_var * merged)
        info_now = merged * shrink
        return info_now, (shrink, info_now)

    zero_info = jnp.zeros(drift_var.shape, dtype=jnp.float32)
    last_info, (shrinks, infos) = lax.scan(backward_step, zero_info, obs_precision[1:], reverse=True)
    shrinks = jnp.concatenate([shrinks, jnp.ones_like(zero_info)[None]], axis=0)
    infos = jnp.concatenate([infos, zero_info[None]], axis=0)
    return gains, filt_vars, shrinks, infos


def e_step(looked, word_counts, topic_prior):
    counts_float = word_counts.astype(jnp.float32)
    doc_topics = topic_prior + jnp.sum(counts_float, axis=-1, keepdims=True) / K
    scores = looked.astype(jnp.float32)
    for sweep in range(EITERS):
        resp = jax.nn.softmax(lax.digamma(doc_topics)[..., None, :] + scores, axis=-1)
        doc_topics = topic_prior + jnp.sum(counts_float[..., None] * resp, axis=-2)
    weighted = (counts_float[..., None] * resp).astype(jnp.bfloat16)
    return doc_topics, weighted


def reference(beta, word_ids, word_counts, block_slot, topic_prior, drift_var, obs_precision):
    normalizer = jax.nn.logsumexp(beta, axis=1, keepdims=True)
    table = (beta - normalizer).astype(jnp.bfloat16)
    columns = (jnp.take(block_slot, word_ids // BLOCK) * BLOCK + word_ids % BLOCK).astype(jnp.int32)
    looked = jax.vmap(lambda table_year, cols_year: jnp.take(table_year, cols_year, axis=0))(table, columns)
    doc_topics, weighted = e_step(looked, word_counts, topic_prior)

    def year_counts(cols_year, weights_year):
        return jax.ops.segment_sum(weights_year.reshape(-1, K).astype(jnp.float32), cols_year.reshape(-1), num_segments=V)

    counts = jax.vmap(year_counts)(columns, weighted)
    pseudo = beta + jnp.log1p(counts)
    gains, filt_vars, shrinks, infos = variance_tables(obs_precision, drift_var)

    def filter_step(mean_prev, inputs):
        gain_now, pseudo_now = inputs
        mean_now = (1.0 - gain_now) * mean_prev + gain_now * pseudo_now
        return mean_now, mean_now

    zero_mean = jnp.zeros(beta.shape[1:], dtype=jnp.float32)
    last_mean, filtered = lax.scan(filter_step, zero_mean, (gains[:, None, :], pseudo))
    pulls = filt_vars / (filt_vars + drift_var)
    pulls = pulls.at[-1].set(0.0)

    def smooth_step(mean_next, inputs):
        pull_now, filt_now = inputs
        mean_now = pull_now * mean_next + (1.0 - pull_now) * filt_now
        return mean_now, mean_now

    first_mean, smoothed = lax.scan(smooth_step, zero_mean, (pulls[:, None, :], filtered), reverse=True)
    return smoothed, doc_topics
```

```python
import functools

import jax
import jax.numpy as jnp
from jax import lax
from jax.experimental import pallas as pl
from jax.experimental.pallas import tpu as pltpu
from jax.sharding import PartitionSpec as P

K = 128
BLOCK = 128
EITERS = 4
GROUP = 4
CHUNKS = 4
INIT_VAR = 4.0
MESH = pl.DeviceIdType.MESH
LINK = jnp.float32


def exp_digamma(x):
    y = x + 6.0
    inv = 1.0 / y
    inv2 = inv * inv
    series = inv * 0.5 + inv2 * (1.0 / 12.0 - inv2 * (1.0 / 120.0 - inv2 * (1.0 / 252.0 - inv2 * (1.0 / 240.0))))
    steps = 1.0 / x
    for i in range(1, 6):
        steps = steps + 1.0 / (x + float(i))
    return y * jnp.exp(-(series + steps))


def send(src, dst, send_sem, recv_sem, where):
    return pltpu.make_async_remote_copy(
        src_ref=src, dst_ref=dst, send_sem=send_sem, recv_sem=recv_sem, device_id=where, device_id_type=MESH
    )


def front_kernel(
    n_doc,
    beta_ref,
    ids_ref,
    cnt_ref,
    slot_ref,
    prior_ref,
    pseudo_ref,
    topics_ref,
    msg,
    land,
    table,
    expo,
    cbro,
    weighted,
    alpha,
    part,
    sums,
    msg_send,
    msg_recv,
    sum_send,
    sum_recv,
):
    me = lax.axis_index("doc")
    own = beta_ref.shape[0]
    dpd = ids_ref.shape[0]
    docs = dpd * n_doc

    def peers():
        return [(off, lax.rem(me + off, n_doc)) for off in range(1, n_doc)]

    barrier = pltpu.get_barrier_semaphore()
    for _, peer in peers():
        pl.semaphore_signal(barrier, inc=1, device_id={"doc": peer}, device_id_type=MESH)

    ids = ids_ref[...]
    block_of = lax.shift_right_logical(ids, 7)
    inside = jnp.bitwise_and(ids, 127)
    place = jnp.zeros_like(ids)
    for b in range(slot_ref.shape[0]):
        place = jnp.where(block_of == b, slot_ref[b], place)
    columns = (place * BLOCK + inside).astype(jnp.float32)
    beta = beta_ref[...]
    peak = jnp.max(beta, axis=0, keepdims=True)
    total = jnp.sum(jnp.exp(beta - peak), axis=0, keepdims=True)
    msg[...] = jnp.zeros_like(msg)
    msg[0:dpd, :] = columns
    msg[dpd : 2 * dpd, :] = cnt_ref[...].astype(jnp.float32)
    msg[2 * dpd : 2 * dpd + 1, :] = peak
    msg[2 * dpd + 1 : 2 * dpd + 2, :] = total
    land[me] = msg[...]

    pl.semaphore_wait(barrier, n_doc - 1)
    for off, peer in peers():
        send(msg, land.at[me], msg_send.at[off], msg_recv.at[me], {"doc": peer}).start()
    for off, peer in peers():
        send(msg, land.at[peer], msg_send.at[off], msg_recv.at[peer], {"doc": peer}).wait_recv()

    peaks = [land[s, 2 * dpd : 2 * dpd + 1, :] for s in range(n_doc)]
    peak = functools.reduce(jnp.maximum, peaks)
    total = sum(land[s, 2 * dpd + 1 : 2 * dpd + 2, :] * jnp.exp(peaks[s] - peak) for s in range(n_doc))
    table[...] = (beta_ref[...] - (peak + jnp.log(total))).astype(jnp.bfloat16)

    base = (me * own).astype(jnp.float32)
    lanes = lax.broadcasted_iota(jnp.int32, (128, 128), 1).astype(jnp.float32)

    def look_up(s, _):
        rows, scales = [], []
        for i in range(dpd):
            col = jnp.transpose(jnp.broadcast_to(land[s, pl.ds(i, 1), :], (128, 128))) - base
            cnt = jnp.transpose(jnp.broadcast_to(land[s, pl.ds(dpd + i, 1), :], (128, 128)))
            rows.append(
                jnp.concatenate(
                    [(col == lanes + float(128 * j)).astype(jnp.bfloat16) for j in range(own // 128)], axis=1
                )
            )
            scales.append(jnp.where((col >= 0.0) & (col < float(own)), cnt, 0.0))
        marks = jnp.concatenate(rows, axis=0)
        looked = jnp.dot(marks, table[...], preferred_element_type=jnp.float32)
        at = pl.ds(pl.multiple_of(s * dpd * 128, dpd * 128), dpd * 128)
        expo[at, :] = jnp.exp(looked - jnp.max(looked, axis=1, keepdims=True))
        cbro[at, :] = jnp.concatenate(scales, axis=0)
        return 0

    lax.fori_loop(0, n_doc, look_up, 0)

    prior = prior_ref[...]
    for s in range(n_doc):
        start = jnp.sum(land[s, dpd : 2 * dpd, :], axis=1, keepdims=True) / K
        alpha[s] = exp_digamma(prior + start)

    for sweep in range(EITERS):
        last = sweep == EITERS - 1

        def e_step(s, _, last=last):
            for i in range(dpd):
                at = pl.ds(pl.multiple_of((s * dpd + i) * 128, 128), 128)
                scaled = expo[at, :] * alpha[s, pl.ds(i, 1), :]
                ratio = cbro[at, :] * (1.0 / jnp.sum(scaled, axis=1, keepdims=True))
                scaled = scaled * ratio
                if last:
                    weighted[at, :] = scaled.astype(jnp.bfloat16)
                part[sweep, s, pl.ds(i, 1), :] = jnp.sum(scaled, axis=0, keepdims=True)
            return 0

        lax.fori_loop(0, n_doc, e_step, 0)
        if not last:
            sums[sweep, me] = part[sweep]
            for off, peer in peers():
                send(
                    part.at[sweep], sums.at[sweep, me], sum_send.at[sweep, off], sum_recv.at[sweep, me], {"doc": peer}
                ).start()
            for off, peer in peers():
                send(
                    part.at[sweep], sums.at[sweep, peer], sum_send.at[sweep, off], sum_recv.at[sweep, peer], {"doc": peer}
                ).wait_recv()
            whole = sums[sweep, 0]
            for s in range(1, n_doc):
                whole = whole + sums[sweep, s]
            alpha[...] = exp_digamma(prior_ref[...] + whole)
        else:
            sums[sweep, me, 0] = part[sweep, me]
            for off, peer in peers():
                send(
                    part.at[sweep, peer],
                    sums.at[sweep, me, 0],
                    sum_send.at[sweep, off],
                    sum_recv.at[sweep, me],
                    {"doc": peer},
                ).start()

    tile = min(own, 512)

    def count(w, _):
        first = pl.multiple_of(w * tile, tile)
        words = (lax.broadcasted_iota(jnp.int32, (tile, 128), 0) + (first + me * own)).astype(jnp.float32)
        marks = jnp.concatenate(
            [(words == land[s, i : i + 1, :]).astype(jnp.bfloat16) for s in range(n_doc) for i in range(dpd)], axis=1
        )
        counts = jnp.dot(marks, weighted[...], preferred_element_type=jnp.float32)
        pseudo_ref[pl.ds(first, tile), :] = beta_ref[pl.ds(first, tile), :] + jnp.log1p(counts)
        return 0

    lax.fori_loop(0, own // tile, count, 0)

    sweep = EITERS - 1
    for off, peer in peers():
        send(
            part.at[sweep, peer], sums.at[sweep, peer, 0], sum_send.at[sweep, off], sum_recv.at[sweep, peer], {"doc": peer}
        ).wait_recv()
    whole = sums[sweep, 0, 0]
    for s in range(1, n_doc):
        whole = whole + sums[sweep, s, 0]
    topics_ref[...] = prior_ref[...] + whole

    for off, peer in peers():
        send(msg, land.at[me], msg_send.at[off], msg_recv.at[me], {"doc": peer}).wait_send()
        for sweep in range(EITERS - 1):
            send(
                part.at[sweep], sums.at[sweep, me], sum_send.at[sweep, off], sum_recv.at[sweep, me], {"doc": peer}
            ).wait_send()
        sweep = EITERS - 1
        send(
            part.at[sweep, peer], sums.at[sweep, me, 0], sum_send.at[sweep, off], sum_recv.at[sweep, me], {"doc": peer}
        ).wait_send()


def smooth_kernel(
    n_tm,
    pseudo_ref,
    prec_ref,
    drift_ref,
    out_ref,
    gain,
    back,
    share,
    years_in,
    local,
    fore,
    hind,
    fore_in,
    hind_in,
    fore_out,
    hind_out,
    years_out,
    in_send,
    in_recv,
    fore_send,
    fore_recv,
    hind_send,
    hind_recv,
    out_send,
    out_recv,
):
    t = lax.axis_index("tm")
    z = t // GROUP
    q = lax.rem(t, GROUP)
    n_z = n_tm // GROUP
    own = pseudo_ref.shape[0]
    span = own // GROUP
    width = span // CHUNKS

    def mates():
        return [(off, lax.rem(q + off, GROUP)) for off in range(1, GROUP)]

    def mate_id(mate):
        return {"tm": z * GROUP + mate}

    barrier = pltpu.get_barrier_semaphore()
    for _, mate in mates():
        pl.semaphore_signal(barrier, inc=1, device_id=mate_id(mate), device_id_type=MESH)

    @pl.when(z > 0)
    def _():
        pl.semaphore_signal(barrier, inc=1, device_id={"tm": t - GROUP}, device_id_type=MESH)

    @pl.when(z < n_z - 1)
    def _():
        pl.semaphore_signal(barrier, inc=1, device_id={"tm": t + GROUP}, device_id_type=MESH)

    pl.semaphore_wait(barrier, GROUP - 1 + jnp.minimum(z, 1) + jnp.minimum(n_z - 1 - z, 1))

    def in_copy(c, off, mate, source):
        return send(
            pseudo_ref.at[pl.ds(pl.multiple_of(mate * span + c * width, width), width), :],
            years_in.at[c, source],
            in_send.at[c, off],
            in_recv.at[c, source],
            mate_id(mate),
        )

    for c in range(CHUNKS):
        for off, mate in mates():
            in_copy(c, off, mate, q).start()

    drift = drift_ref[...]
    var = jnp.full_like(drift, INIT_VAR)
    filt = []
    for k in range(n_tm):
        precision = prec_ref[k : k + 1, :]
        inverse = 1.0 / (1.0 + var * precision)
        gain[k : k + 1, :] = var * precision * inverse
        filt.append(var * inverse)
        var = filt[k] + drift
    info = jnp.zeros_like(drift)
    for k in reversed(range(n_tm)):
        share[k : k + 1, :] = 1.0 / (1.0 + filt[k] * info)
        precision = prec_ref[k : k + 1, :]
        merged = info + precision
        back[k : k + 1, :] = precision / merged
        info = merged / (1.0 + drift * merged)

    g = [gain[pl.ds(z * GROUP + i, 1), :] for i in range(GROUP)]
    r = [back[pl.ds(z * GROUP + i, 1), :] for i in range(GROUP)]
    w = [share[pl.ds(z * GROUP + i, 1), :] for i in range(GROUP)]
    keep = []
    for i in range(GROUP):
        keep.append((1.0 - g[i]) * keep[-1] if i else 1.0 - g[i])
    hold = [jnp.ones_like(g[0])]
    for i in reversed(range(GROUP)):
        hold.insert(0, (1.0 - r[i]) * hold[0])

    def fore_copy(c):
        return send(fore_out.at[c], fore_in.at[c], fore_send.at[c], fore_recv.at[c], {"tm": t + GROUP})

    def hind_copy(c):
        return send(hind_out.at[c], hind_in.at[c], hind_send.at[c], hind_recv.at[c], {"tm": t - GROUP})

    def fore_arrived(c):
        send(fore_out.at[c], fore_in.at[c], fore_send.at[c], fore_recv.at[c], {"tm": t - GROUP}).wait_recv()

    def hind_arrived(c):
        send(hind_out.at[c], hind_in.at[c], hind_send.at[c], hind_recv.at[c], {"tm": t + GROUP}).wait_recv()

    for c in range(CHUNKS):
        years_in[c, q] = pseudo_ref[pl.ds(pl.multiple_of(q * span + c * width, width), width), :].astype(LINK)
        for off, mate in mates():
            in_copy(c, off, mate, mate).wait_recv()
        values = [years_in[c, i].astype(jnp.float32) for i in range(GROUP)]
        ahead = []
        for i in range(GROUP):
            ahead.append(g[i] * values[i] + ((1.0 - g[i]) * ahead[-1] if i else 0.0))
        fore[c] = ahead[-1]
        behind = r[GROUP - 1] * values[GROUP - 1]
        local[c, GROUP - 1] = w[GROUP - 1] * ahead[GROUP - 1]
        for i in reversed(range(GROUP - 1)):
            local[c, i] = w[i] * ahead[i] + (1.0 - w[i]) * behind
            behind = r[i] * values[i] + (1.0 - r[i]) * behind
        hind[c] = behind

        @pl.when(z == 0)
        def _():
            fore_in[c] = jnp.zeros_like(fore_in.at[c])
            fore_out[c] = fore[c].astype(LINK)
            fore_copy(c).start()

        @pl.when(z == n_z - 1)
        def _():
            hind_in[c] = jnp.zeros_like(hind_in.at[c])
            hind_out[c] = hind[c].astype(LINK)
            hind_copy(c).start()

    def do_fore(c):
        @pl.when(z > 0)
        def _():
            fore_arrived(c)

        @pl.when((z > 0) & (z < n_z - 1))
        def _():
            fore_out[c] = (keep[-1] * fore_in[c].astype(jnp.float32) + fore[c]).astype(LINK)
            fore_copy(c).start()

    def do_hind(c):
        @pl.when(z < n_z - 1)
        def _():
            hind_arrived(c)

        @pl.when((z > 0) & (z < n_z - 1))
        def _():
            hind_out[c] = (hold[0] * hind_in[c].astype(jnp.float32) + hind[c]).astype(LINK)
            hind_copy(c).start()

    def out_rows(source, c):
        return pl.ds(pl.multiple_of(source * span + c * width, width), width)

    def out_copy(c, off, mate, source):
        return send(
            years_out.at[c, mate], out_ref.at[out_rows(source, c), :], out_send.at[c, off], out_recv.at[c, source], mate_id(mate)
        )

    def finish(c):
        ahead = fore_in[c].astype(jnp.float32)
        behind = hind_in[c].astype(jnp.float32)
        for i in range(GROUP):
            years_out[c, i] = local[c, i] + (w[i] * keep[i]) * ahead + ((1.0 - w[i]) * hold[i + 1]) * behind
        for off, mate in mates():
            out_copy(c, off, mate, q).start()
        out_ref[out_rows(q, c), :] = years_out[c, q]

    early = z < n_z // 2
    lead = jnp.where(early, n_z - 1 - 2 * z, 2 * z + 1 - n_z)

    def step(k, _):
        @pl.when(k < CHUNKS)
        def _():
            @pl.when(early)
            def _():
                do_fore(k)

            @pl.when(jnp.logical_not(early))
            def _():
                do_hind(k)

        late = k - lead

        @pl.when(late >= 0)
        def _():
            @pl.when(early)
            def _():
                do_hind(late)

            @pl.when(jnp.logical_not(early))
            def _():
                do_fore(late)

            finish(late)

        return 0

    lax.fori_loop(0, CHUNKS + lead, step, 0)

    for c in range(CHUNKS):
        for off, mate in mates():
            out_copy(c, off, mate, mate).wait_recv()
    for c in range(CHUNKS):
        for off, mate in mates():
            in_copy(c, off, mate, q).wait_send()
            out_copy(c, off, mate, q).wait_send()

        @pl.when(z < n_z - 1)
        def _():
            fore_copy(c).wait_send()

        @pl.when(z > 0)
        def _():
            hind_copy(c).wait_send()


def vmem():
    return pl.BlockSpec(memory_space=pltpu.VMEM)


def solution(mesh):
    n_tm, n_doc = mesh.shape["tm"], mesh.shape["doc"]

    def body(beta, word_ids, word_counts, block_slot, topic_prior, drift_var, obs_precision):
        local_beta, ids, cnt = beta[0], word_ids[0], word_counts[0]
        own, dpd = local_beta.shape[0], ids.shape[0]
        slots = dpd * n_doc * 128
        f32, bf16 = jnp.float32, jnp.bfloat16
        dma = pltpu.SemaphoreType.DMA
        pseudo, doc_topics = pl.pallas_call(
            functools.partial(front_kernel, n_doc),
            out_shape=(jax.ShapeDtypeStruct((own, K), f32), jax.ShapeDtypeStruct((dpd, K), f32)),
            in_specs=[vmem(), vmem(), vmem(), pl.BlockSpec(memory_space=pltpu.SMEM), vmem()],
            out_specs=(vmem(), vmem()),
            scratch_shapes=[
                pltpu.VMEM((16, K), f32),
                pltpu.VMEM((n_doc, 16, K), f32),
                pltpu.VMEM((own, K), bf16),
                pltpu.VMEM((slots, K), f32),
                pltpu.VMEM((slots, K), f32),
                pltpu.VMEM((slots, K), bf16),
                pltpu.VMEM((n_doc, dpd, K), f32),
                pltpu.VMEM((EITERS, n_doc, dpd, K), f32),
                pltpu.VMEM((EITERS, n_doc, n_doc, dpd, K), f32),
                dma((n_doc,)),
                dma((n_doc,)),
                dma((EITERS, n_doc)),
                dma((EITERS, n_doc)),
            ],
            compiler_params=pltpu.CompilerParams(
                collective_id=0, has_side_effects=True, vmem_limit_bytes=48 * 1024 * 1024
            ),
            name="estep",
        )(local_beta, ids, cnt, block_slot, topic_prior[None])
        width = own // GROUP // CHUNKS
        smoothed = pl.pallas_call(
            functools.partial(smooth_kernel, n_tm),
            out_shape=jax.ShapeDtypeStruct((own, K), f32),
            in_specs=[vmem(), vmem(), vmem()],
            out_specs=vmem(),
            scratch_shapes=[
                pltpu.VMEM((n_tm, K), f32),
                pltpu.VMEM((n_tm, K), f32),
                pltpu.VMEM((n_tm, K), f32),
                pltpu.VMEM((CHUNKS, GROUP, width, K), LINK),
                pltpu.VMEM((CHUNKS, GROUP, width, K), f32),
                pltpu.VMEM((CHUNKS, width, K), f32),
                pltpu.VMEM((CHUNKS, width, K), f32),
                pltpu.VMEM((CHUNKS, width, K), LINK),
                pltpu.VMEM((CHUNKS, width, K), LINK),
                pltpu.VMEM((CHUNKS, width, K), LINK),
                pltpu.VMEM((CHUNKS, width, K), LINK),
                pltpu.VMEM((CHUNKS, GROUP, width, K), LINK),
                dma((CHUNKS, GROUP)),
                dma((CHUNKS, GROUP)),
                dma((CHUNKS,)),
                dma((CHUNKS,)),
                dma((CHUNKS,)),
                dma((CHUNKS,)),
                dma((CHUNKS, GROUP)),
                dma((CHUNKS, GROUP)),
            ],
            compiler_params=pltpu.CompilerParams(
                collective_id=1, has_side_effects=True, vmem_limit_bytes=48 * 1024 * 1024
            ),
            name="smooth",
        )(pseudo, obs_precision, drift_var[None])
        return (smoothed[None], doc_topics[None])

    in_specs = (P("tm", "doc", None), P("tm", "doc", None), P("tm", "doc", None), P(), P(), P(), P())
    out_specs = (P("tm", "doc", None), P("tm", "doc", None))
    return jax.shard_map(body, mesh=mesh, in_specs=in_specs, out_specs=out_specs, check_vma=False)
```

```python
import functools

import jax
import jax.numpy as jnp
from jax import lax
from jax.experimental import pallas as pl
from jax.experimental.pallas import tpu as pltpu
from jax.sharding import PartitionSpec as P

K = 128
BLOCK = 128
EITERS = 4
GROUP = 8
CHUNKS = 2
INIT_VAR = 4.0
MESH = pl.DeviceIdType.MESH


def exp_digamma(x):
    u = x * (x + 5.0)
    steps = (2.0 * x + 5.0) * ((3.0 * u + 20.0) * u + 24.0) / (u * (u + 4.0) * (u + 6.0))
    y = x + 6.0
    inv = 1.0 / y
    inv2 = inv * inv
    series = inv * 0.5 + inv2 * (1.0 / 12.0 - inv2 * (1.0 / 120.0 - inv2 * (1.0 / 252.0 - inv2 * (1.0 / 240.0))))
    return y * jnp.exp(-(series + steps))


def send(src, dst, send_sem, recv_sem, where):
    return pltpu.make_async_remote_copy(
        src_ref=src, dst_ref=dst, send_sem=send_sem, recv_sem=recv_sem, device_id=where, device_id_type=MESH
    )


def kernel(
    n_tm,
    n_doc,
    beta_ref,
    ids_ref,
    cnt_ref,
    slot_ref,
    prior_ref,
    prec_ref,
    drift_ref,
    out_ref,
    topics_ref,
    msg,
    land,
    table,
    rows_out,
    rows_in,
    expo,
    weighted,
    counts,
    gain,
    back,
    share,
    pseudo,
    years_in,
    local,
    mid_out,
    mid_in,
    years_out,
    msg_send,
    msg_recv,
    row_send,
    row_recv,
    wgt_send,
    wgt_recv,
    in_send,
    in_recv,
    mid_send,
    mid_recv,
    out_send,
    out_recv,
):
    me = lax.axis_index("doc")
    t = lax.axis_index("tm")
    n_blocks = n_tm // GROUP
    b = t // GROUP
    m = lax.rem(t, GROUP)
    own = beta_ref.shape[0]
    dpd = ids_ref.shape[0]
    held = dpd * 128
    span = own // GROUP
    width = span // CHUNKS

    peers = [(off, lax.rem(me + off, n_doc)) for off in range(1, n_doc)]
    mates = [(off, lax.rem(m + off, GROUP)) for off in range(1, GROUP)]
    others = [(off, lax.rem(b + off, n_blocks)) for off in range(1, n_blocks)]

    def mate_id(mate):
        return {"tm": b * GROUP + mate}

    def other_id(other):
        return {"tm": other * GROUP + m}

    barrier = pltpu.get_barrier_semaphore()
    for _, peer in peers:
        pl.semaphore_signal(barrier, inc=1, device_id={"doc": peer}, device_id_type=MESH)
    for _, mate in mates:
        pl.semaphore_signal(barrier, inc=1, device_id=mate_id(mate), device_id_type=MESH)
    for _, other in others:
        pl.semaphore_signal(barrier, inc=1, device_id=other_id(other), device_id_type=MESH)

    ids = ids_ref[...]
    block_of = lax.shift_right_logical(ids, 7)
    inside = jnp.bitwise_and(ids, 127)
    place = jnp.zeros_like(ids)
    for k in range(slot_ref.shape[0]):
        place = jnp.where(block_of == k, slot_ref[k], place)
    columns = (place * BLOCK + inside).astype(jnp.float32)
    beta = beta_ref[...]
    peak = jnp.max(beta, axis=0, keepdims=True)
    total = jnp.sum(jnp.exp(beta - peak), axis=0, keepdims=True)
    msg[...] = jnp.zeros_like(msg)
    msg[0:dpd, :] = columns
    msg[dpd : dpd + 1, :] = peak
    msg[dpd + 1 : dpd + 2, :] = total
    land[me] = msg[...]

    pl.semaphore_wait(barrier, len(peers) + len(mates) + len(others))

    def msg_copy(off, peer, source):
        return send(msg, land.at[source], msg_send.at[off], msg_recv.at[source], {"doc": peer})

    for off, peer in peers:
        msg_copy(off, peer, me).start()

    drift = drift_ref[...]
    var = jnp.full_like(drift, INIT_VAR)
    filt = []
    for k in range(n_tm):
        precision = prec_ref[k : k + 1, :]
        inverse = 1.0 / (1.0 + var * precision)
        gain[k : k + 1, :] = var * precision * inverse
        filt.append(var * inverse)
        var = filt[k] + drift
    info = jnp.zeros_like(drift)
    for k in reversed(range(n_tm)):
        share[k : k + 1, :] = 1.0 / (1.0 + filt[k] * info)
        precision = prec_ref[k : k + 1, :]
        merged = info + precision
        back[k : k + 1, :] = precision / merged
        info = merged / (1.0 + drift * merged)
    cnt = cnt_ref[...].astype(jnp.float32)
    scale = [jnp.transpose(jnp.broadcast_to(cnt[i : i + 1, :], (128, 128))) for i in range(dpd)]
    prior = prior_ref[...]
    alpha = exp_digamma(prior + jnp.sum(cnt, axis=1, keepdims=True) / K)

    for off, peer in peers:
        msg_copy(off, peer, peer).wait_recv()

    peaks = [land[s, dpd : dpd + 1, :] for s in range(n_doc)]
    peak = functools.reduce(jnp.maximum, peaks)
    total = sum(land[s, dpd + 1 : dpd + 2, :] * jnp.exp(peaks[s] - peak) for s in range(n_doc))
    table[...] = (beta_ref[...] - (peak + jnp.log(total))).astype(jnp.bfloat16)

    base = (me * own).astype(jnp.float32)
    lanes = lax.broadcasted_iota(jnp.int32, (128, 128), 1).astype(jnp.float32)

    def row_copy(peer, source):
        return send(rows_out.at[peer], rows_in.at[source], row_send.at[peer], row_recv.at[source], {"doc": peer})

    def look_up(k, _):
        s = lax.rem(me + 3 * (k + 1), n_doc)
        marks = []
        for i in range(dpd):
            col = jnp.transpose(jnp.broadcast_to(land[s, pl.ds(i, 1), :], (128, 128))) - base
            marks.append(
                jnp.concatenate(
                    [(col == lanes + float(128 * j)).astype(jnp.bfloat16) for j in range(own // 128)], axis=1
                )
            )
        looked = jnp.dot(jnp.concatenate(marks, axis=0), table[...], preferred_element_type=jnp.float32)
        rows_out[s] = looked.astype(jnp.bfloat16)

        @pl.when(k < n_doc - 1)
        def _():
            row_copy(s, me).start()

        return 0

    lax.fori_loop(0, n_doc, look_up, 0)
    rows_in[me] = rows_out[me]
    for _, peer in peers:
        row_copy(peer, peer).wait_recv()

    for i in range(dpd):
        at = slice(i * 128, (i + 1) * 128)
        looked = rows_in[0, at, :].astype(jnp.float32)
        for s in range(1, n_doc):
            looked = looked + rows_in[s, at, :].astype(jnp.float32)
        expo[at, :] = jnp.exp(looked - jnp.max(looked, axis=1, keepdims=True))
    for sweep in range(EITERS):
        sums = []
        for i in range(dpd):
            at = slice(i * 128, (i + 1) * 128)
            scaled = expo[at, :] * alpha[i : i + 1, :]
            scaled = scaled * (scale[i] * (1.0 / jnp.sum(scaled, axis=1, keepdims=True)))
            if sweep == EITERS - 1:
                weighted[me, at, :] = scaled.astype(jnp.bfloat16)
            sums.append(jnp.sum(scaled, axis=0, keepdims=True))
        topics = prior + jnp.concatenate(sums, axis=0)
        if sweep < EITERS - 1:
            alpha = exp_digamma(topics)

    def wgt_copy(off, peer, source):
        return send(weighted.at[source], weighted.at[source], wgt_send.at[off], wgt_recv.at[source], {"doc": peer})

    for off, peer in sorted(peers, key=lambda p: abs(p[0] - n_doc // 2)):
        wgt_copy(off, peer, me).start()
    topics_ref[...] = topics

    def tally(s, first, length):
        words = (lax.broadcasted_iota(jnp.int32, (length, 128), 0) + (first + me * own)).astype(jnp.float32)
        marks = jnp.concatenate(
            [(words == land[s, i : i + 1, :]).astype(jnp.bfloat16) for i in range(dpd)], axis=1
        )
        return jnp.dot(marks, weighted[s], preferred_element_type=jnp.float32)

    tile = min(own, 512)

    def first_tally(w, _):
        first = pl.multiple_of(w * tile, tile)
        counts[pl.ds(first, tile), :] = tally(me, first, tile)
        return 0

    lax.fori_loop(0, own // tile, first_tally, 0)
    arrival = sorted(peers, key=lambda p: -abs(p[0] - n_doc // 2))
    for off, peer in arrival[:-1]:
        wgt_copy(off, peer, peer).wait_recv()

        def more_tally(w, _, peer=peer):
            first = pl.multiple_of(w * tile, tile)
            counts[pl.ds(first, tile), :] += tally(peer, first, tile)
            return 0

        lax.fori_loop(0, own // tile, more_tally, 0)
    off, final = arrival[-1]
    wgt_copy(off, final, final).wait_recv()

    def word_rows(mate, c):
        return pl.ds(pl.multiple_of(mate * span + c * width, width), width)

    def in_copy(c, mate, source):
        return send(
            pseudo.at[word_rows(mate, c), :], years_in.at[c, source], in_send.at[c, mate], in_recv.at[c, source], mate_id(mate)
        )

    def last_tally(k, _):
        c = k // GROUP
        mate = lax.rem(m + 1 + lax.rem(k, GROUP), GROUP)
        at = word_rows(mate, c)
        whole = counts[at, :] + tally(final, mate * span + c * width, width)
        pseudo[at, :] = beta_ref[at, :] + jnp.log1p(whole)

        @pl.when(mate != m)
        def _():
            in_copy(c, mate, m).start()

        return 0

    lax.fori_loop(0, CHUNKS * GROUP, last_tally, 0)

    first_year = b * GROUP
    g = [gain[pl.ds(first_year + i, 1), :] for i in range(GROUP)]
    r = [back[pl.ds(first_year + i, 1), :] for i in range(GROUP)]
    w = [share[pl.ds(first_year + i, 1), :] for i in range(GROUP)]
    keep = []
    for i in range(GROUP):
        keep.append((1.0 - g[i]) * keep[-1] if i else 1.0 - g[i])
    hold = [jnp.ones_like(g[0])]
    for i in reversed(range(GROUP)):
        hold.insert(0, (1.0 - r[i]) * hold[0])
    block_keep, block_hold = [], []
    for other in range(n_blocks):
        years = range(other * GROUP, (other + 1) * GROUP)
        block_keep.append(functools.reduce(jnp.multiply, [1.0 - gain[y : y + 1, :] for y in years]))
        block_hold.append(functools.reduce(jnp.multiply, [1.0 - back[y : y + 1, :] for y in years]))
    into = []
    for other in range(n_blocks):
        fore = jnp.where(other < b, 1.0, 0.0)
        for between in range(other + 1, n_blocks):
            fore = fore * jnp.where(between < b, block_keep[between], 1.0)
        hind = jnp.where(other > b, 1.0, 0.0)
        for between in range(other):
            hind = hind * jnp.where(between > b, block_hold[between], 1.0)
        into.append((fore, hind))

    def mid_copy(c, off, other, source):
        which = jnp.where(other > b, 0, 1)
        return send(mid_out.at[c, which], mid_in.at[c, source], mid_send.at[c, off], mid_recv.at[c, source], other_id(other))

    for c in range(CHUNKS):
        years_in[c, m] = pseudo[word_rows(m, c), :]
        mid_in[c, b] = jnp.zeros((width, K), jnp.float32)
        for off, mate in mates:
            in_copy(c, mate, mate).wait_recv()
        ahead = g[0] * years_in[c, 0]
        local[c, 0] = w[0] * ahead
        for i in range(1, GROUP):
            ahead = g[i] * years_in[c, i] + (1.0 - g[i]) * ahead
            local[c, i] = w[i] * ahead
        mid_out[c, 0] = ahead
        behind = r[GROUP - 1] * years_in[c, GROUP - 1]
        for i in reversed(range(GROUP - 1)):
            local[c, i] += (1.0 - w[i]) * behind
            behind = r[i] * years_in[c, i] + (1.0 - r[i]) * behind
        mid_out[c, 1] = behind
        for off, other in others:
            mid_copy(c, off, other, b).start()

    def out_copy(c, mate, source):
        return send(
            years_out.at[c, mate], out_ref.at[word_rows(source, c), :], out_send.at[c, mate], out_recv.at[c, source], mate_id(mate)
        )

    for c in range(CHUNKS):
        for off, other in others:
            mid_copy(c, off, other, other).wait_recv()
        ahead, behind = 0.0, 0.0
        for other in range(n_blocks):
            value = mid_in[c, other]
            ahead = ahead + into[other][0] * value
            behind = behind + into[other][1] * value
        for i in range(GROUP):
            years_out[c, i] = local[c, i] + (w[i] * keep[i]) * ahead + ((1.0 - w[i]) * hold[i + 1]) * behind
        for off, mate in mates:
            out_copy(c, mate, m).start()
        out_ref[word_rows(m, c), :] = years_out[c, m]

    for c in range(CHUNKS):
        for off, mate in mates:
            out_copy(c, mate, mate).wait_recv()
    for off, peer in peers:
        msg_copy(off, peer, me).wait_send()
        row_copy(peer, me).wait_send()
        wgt_copy(off, peer, me).wait_send()
    for c in range(CHUNKS):
        for off, mate in mates:
            in_copy(c, mate, m).wait_send()
            out_copy(c, mate, m).wait_send()
        for off, other in others:
            mid_copy(c, off, other, b).wait_send()


def vmem():
    return pl.BlockSpec(memory_space=pltpu.VMEM)


def solution(mesh):
    n_tm, n_doc = mesh.shape["tm"], mesh.shape["doc"]

    def body(beta, word_ids, word_counts, block_slot, topic_prior, drift_var, obs_precision):
        local_beta, ids, cnt = beta[0], word_ids[0], word_counts[0]
        own, dpd = local_beta.shape[0], ids.shape[0]
        held = dpd * 128
        width = own // GROUP // CHUNKS
        n_blocks = n_tm // GROUP
        f32, bf16 = jnp.float32, jnp.bfloat16
        dma = pltpu.SemaphoreType.DMA
        smoothed, doc_topics = pl.pallas_call(
            functools.partial(kernel, n_tm, n_doc),
            out_shape=(jax.ShapeDtypeStruct((own, K), f32), jax.ShapeDtypeStruct((dpd, K), f32)),
            in_specs=[vmem(), vmem(), vmem(), pl.BlockSpec(memory_space=pltpu.SMEM), vmem(), vmem(), vmem()],
            out_specs=(vmem(), vmem()),
            scratch_shapes=[
                pltpu.VMEM((8, K), f32),
                pltpu.VMEM((n_doc, 8, K), f32),
                pltpu.VMEM((own, K), bf16),
                pltpu.VMEM((n_doc, held, K), bf16),
                pltpu.VMEM((n_doc, held, K), bf16),
                pltpu.VMEM((held, K), f32),
                pltpu.VMEM((n_doc, held, K), bf16),
                pltpu.VMEM((own, K), f32),
                pltpu.VMEM((n_tm, K), f32),
                pltpu.VMEM((n_tm, K), f32),
                pltpu.VMEM((n_tm, K), f32),
                pltpu.VMEM((own, K), f32),
                pltpu.VMEM((CHUNKS, GROUP, width, K), f32),
                pltpu.VMEM((CHUNKS, GROUP, width, K), f32),
                pltpu.VMEM((CHUNKS, 2, width, K), f32),
                pltpu.VMEM((CHUNKS, n_blocks, width, K), f32),
                pltpu.VMEM((CHUNKS, GROUP, width, K), f32),
                dma((n_doc,)),
                dma((n_doc,)),
                dma((n_doc,)),
                dma((n_doc,)),
                dma((n_doc,)),
                dma((n_doc,)),
                dma((CHUNKS, GROUP)),
                dma((CHUNKS, GROUP)),
                dma((CHUNKS, n_blocks)),
                dma((CHUNKS, n_blocks)),
                dma((CHUNKS, GROUP)),
                dma((CHUNKS, GROUP)),
            ],
            compiler_params=pltpu.CompilerParams(
                collective_id=0, has_side_effects=True, vmem_limit_bytes=48 * 1024 * 1024
            ),
            name="topics",
        )(local_beta, ids, cnt, block_slot, topic_prior[None], obs_precision, drift_var[None])
        return (smoothed[None], doc_topics[None])

    in_specs = (P("tm", "doc", None), P("tm", "doc", None), P("tm", "doc", None), P(), P(), P(), P())
    out_specs = (P("tm", "doc", None), P("tm", "doc", None))
    return jax.shard_map(body, mesh=mesh, in_specs=in_specs, out_specs=out_specs, check_vma=False)
```

```python
import functools

import jax
import jax.numpy as jnp
from jax import lax
from jax.experimental import pallas as pl
from jax.experimental.pallas import tpu as pltpu
from jax.sharding import PartitionSpec as P

K = 128
BLOCK = 128
EITERS = 4
GROUP = 8
FOLD = 4
CHUNKS = 2
INIT_VAR = 4.0
MESH = pl.DeviceIdType.MESH


def exp_digamma(x):
    u = x * (x + 5.0)
    steps = (2.0 * x + 5.0) * ((3.0 * u + 20.0) * u + 24.0) / (u * (u + 4.0) * (u + 6.0))
    y = x + 6.0
    inv = 1.0 / y
    inv2 = inv * inv
    series = inv * 0.5 + inv2 * (1.0 / 12.0 - inv2 * (1.0 / 120.0 - inv2 * (1.0 / 252.0 - inv2 * (1.0 / 240.0))))
    return y * jnp.exp(-(series + steps))


def send(src, dst, send_sem, recv_sem, where):
    return pltpu.make_async_remote_copy(
        src_ref=src, dst_ref=dst, send_sem=send_sem, recv_sem=recv_sem, device_id=where, device_id_type=MESH
    )


def kernel(
    n_tm,
    n_doc,
    beta_ref,
    ids_ref,
    cnt_ref,
    slot_ref,
    prior_ref,
    prec_ref,
    drift_ref,
    out_ref,
    topics_ref,
    msg,
    land,
    table,
    expo,
    scale,
    quarter,
    weighted,
    alpha,
    part,
    sums,
    end_part,
    end_sums,
    gain,
    back,
    share,
    pseudo,
    years_in,
    local,
    mid_out,
    mid_in,
    years_out,
    msg_send,
    msg_recv,
    sum_send,
    sum_recv,
    end_send,
    end_recv,
    in_send,
    in_recv,
    mid_send,
    mid_recv,
    out_send,
    out_recv,
):
    me = lax.axis_index("doc")
    t = lax.axis_index("tm")
    n_blocks = n_tm // GROUP
    b = t // GROUP
    m = lax.rem(t, GROUP)
    own = beta_ref.shape[0]
    dpd = ids_ref.shape[0]
    held = dpd * 128
    span = own // GROUP
    width = span // CHUNKS

    peers = [(off, lax.rem(me + off, n_doc)) for off in range(1, n_doc)]
    mates = [(off, lax.rem(m + off, GROUP)) for off in range(1, GROUP)]
    others = [(off, lax.rem(b + off, n_blocks)) for off in range(1, n_blocks)]

    def mate_id(mate):
        return {"tm": b * GROUP + mate}

    def other_id(other):
        return {"tm": other * GROUP + m}

    barrier = pltpu.get_barrier_semaphore()
    for _, peer in peers:
        pl.semaphore_signal(barrier, inc=1, device_id={"doc": peer}, device_id_type=MESH)
    for _, mate in mates:
        pl.semaphore_signal(barrier, inc=1, device_id=mate_id(mate), device_id_type=MESH)
    for _, other in others:
        pl.semaphore_signal(barrier, inc=1, device_id=other_id(other), device_id_type=MESH)

    ids = ids_ref[...]
    block_of = lax.shift_right_logical(ids, 7)
    inside = jnp.bitwise_and(ids, 127)
    place = jnp.zeros_like(ids)
    for k in range(slot_ref.shape[0]):
        place = jnp.where(block_of == k, slot_ref[k], place)
    columns = (place * BLOCK + inside).astype(jnp.float32)
    beta = beta_ref[...]
    peak = jnp.max(beta, axis=0, keepdims=True)
    total = jnp.sum(jnp.exp(beta - peak), axis=0, keepdims=True)
    msg[...] = jnp.zeros_like(msg)
    msg[0:dpd, :] = columns
    msg[dpd : dpd + 1, :] = peak
    msg[dpd + 1 : dpd + 2, :] = total
    msg[8 : 8 + dpd, :] = cnt_ref[...].astype(jnp.float32)
    land[me] = msg[...]

    pl.semaphore_wait(barrier, len(peers) + len(mates) + len(others))

    def msg_copy(off, peer, source):
        return send(msg, land.at[source], msg_send.at[off], msg_recv.at[source], {"doc": peer})

    for off, peer in peers:
        msg_copy(off, peer, me).start()

    drift = drift_ref[...]
    var = jnp.full_like(drift, INIT_VAR)
    filt = []
    for k in range(n_tm):
        precision = prec_ref[k : k + 1, :]
        inverse = 1.0 / (1.0 + var * precision)
        gain[k : k + 1, :] = var * precision * inverse
        filt.append(var * inverse)
        var = filt[k] + drift
    info = jnp.zeros_like(drift)
    for k in reversed(range(n_tm)):
        share[k : k + 1, :] = 1.0 / (1.0 + filt[k] * info)
        precision = prec_ref[k : k + 1, :]
        merged = info + precision
        back[k : k + 1, :] = precision / merged
        info = merged / (1.0 + drift * merged)
    prior = prior_ref[...]

    for off, peer in peers:
        msg_copy(off, peer, peer).wait_recv()

    peaks = [land[s, dpd : dpd + 1, :] for s in range(n_doc)]
    peak = functools.reduce(jnp.maximum, peaks)
    total = sum(land[s, dpd + 1 : dpd + 2, :] * jnp.exp(peaks[s] - peak) for s in range(n_doc))
    normalizer = peak + jnp.log(total)
    fold = own // FOLD
    for f in range(FOLD):
        table[:, f * K : (f + 1) * K] = (beta_ref[f * fold : (f + 1) * fold, :] - normalizer).astype(jnp.bfloat16)

    base = (me * own).astype(jnp.float32)
    lanes = lax.broadcasted_iota(jnp.int32, (128, 128), 1).astype(jnp.float32)

    for s in range(n_doc):
        start = jnp.sum(land[s, 8 : 8 + dpd, :], axis=1, keepdims=True) / K
        alpha[s * dpd : (s + 1) * dpd, :] = jnp.broadcast_to(start, (dpd, K))
    alpha[...] = exp_digamma(prior + alpha[...])

    def look_up(s, _):
        marks, parts = [], []
        for i in range(dpd):
            both = land[s, pl.ds(i, 1), :] * 16.0 + land[s, pl.ds(8 + i, 1), :]
            both = jnp.transpose(jnp.broadcast_to(both, (128, 128)))
            col = jnp.floor(both * (1.0 / 16.0))
            cnt = both - 16.0 * col
            col = col - base
            part_of = jnp.floor(col * (1.0 / fold))
            rest = col - float(fold) * part_of
            parts.append(part_of)
            at = pl.ds(pl.multiple_of((s * dpd + i) * 128, 128), 128)
            scale[at, :] = jnp.where((part_of >= 0.0) & (part_of < float(FOLD)), cnt, 0.0)
            quarter[at, :] = part_of
            marks.append(
                jnp.concatenate(
                    [(rest == lanes + float(128 * j)).astype(jnp.bfloat16) for j in range(fold // 128)], axis=1
                )
            )
        wide = jnp.dot(jnp.concatenate(marks, axis=0), table[...], preferred_element_type=jnp.float32)
        part_of = jnp.concatenate(parts, axis=0)
        looked = wide[:, 0:K]
        for f in range(1, FOLD):
            looked = jnp.where(part_of == float(f), wide[:, f * K : (f + 1) * K], looked)
        at = pl.ds(pl.multiple_of(s * held, held), held)
        expo[at, :] = jnp.exp(looked - jnp.max(looked, axis=1, keepdims=True))
        return 0

    lax.fori_loop(0, n_doc, look_up, 0)

    def sum_copy(sweep, off, peer, source):
        return send(part.at[sweep], sums.at[sweep, source], sum_send.at[sweep, off], sum_recv.at[sweep, source], {"doc": peer})

    def end_copy(off, peer, source):
        return send(end_part.at[peer], end_sums.at[source], end_send.at[off], end_recv.at[source], {"doc": peer})

    for sweep in range(EITERS):
        last = sweep == EITERS - 1

        def e_step(s, _, last=last, sweep=sweep):
            for i in range(dpd):
                row = s * dpd + i
                at = pl.ds(pl.multiple_of(row * 128, 128), 128)
                scaled = expo[at, :] * alpha[pl.ds(row, 1), :]
                scaled = scaled * (scale[at, :] * (1.0 / jnp.sum(scaled, axis=1, keepdims=True)))
                if last:
                    end_part[s, i : i + 1, :] = jnp.sum(scaled, axis=0, keepdims=True)
                    for f in range(FOLD):
                        weighted[at, f * K : (f + 1) * K] = jnp.where(quarter[at, :] == float(f), scaled, 0.0).astype(
                            jnp.bfloat16
                        )
                else:
                    part[sweep, pl.ds(row, 1), :] = jnp.sum(scaled, axis=0, keepdims=True)
            return 0

        lax.fori_loop(0, n_doc, e_step, 0)
        if not last:
            for off, peer in peers:
                sum_copy(sweep, off, peer, me).start()
            sums[sweep, me] = part[sweep]
            for off, peer in peers:
                sum_copy(sweep, off, peer, peer).wait_recv()
            whole = sums[sweep, 0]
            for s in range(1, n_doc):
                whole = whole + sums[sweep, s]
            alpha[...] = exp_digamma(prior + whole)
        else:
            for off, peer in peers:
                end_copy(off, peer, me).start()
            end_sums[me] = end_part[me]

    def word_rows(mate, c):
        return pl.ds(pl.multiple_of(mate * span + c * width, width), width)

    def in_copy(c, mate, source):
        return send(
            pseudo.at[word_rows(mate, c), :], years_in.at[c, source], in_send.at[c, mate], in_recv.at[c, source], mate_id(mate)
        )

    spans = fold // span
    rests = []
    for s in range(n_doc):
        col = land[s, 0:dpd, :] - base
        rests.append(col - float(fold) * jnp.floor(col * (1.0 / fold)))
    words = lax.broadcasted_iota(jnp.int32, (width, 128), 0).astype(jnp.float32)
    for c in range(CHUNKS):
        marks = []
        for s in range(n_doc):
            for i in range(dpd):
                marks.append(
                    jnp.concatenate(
                        [
                            (words + float(h * span + c * width) == rests[s][i : i + 1, :]).astype(jnp.bfloat16)
                            for h in range(spans)
                        ],
                        axis=0,
                    )
                )
        counts = jnp.dot(jnp.concatenate(marks, axis=1), weighted[...], preferred_element_type=jnp.float32)
        for h in range(spans):
            for f in range(FOLD):
                mate = f * spans + h
                first = mate * span + c * width
                whole = counts[h * width : (h + 1) * width, f * K : (f + 1) * K]
                pseudo[first : first + width, :] = beta_ref[first : first + width, :] + jnp.log1p(whole)

                @pl.when(mate != m)
                def _(mate=mate, c=c):
                    in_copy(c, mate, m).start()

    for off, peer in peers:
        end_copy(off, peer, peer).wait_recv()
    whole = end_sums[0]
    for s in range(1, n_doc):
        whole = whole + end_sums[s]
    topics_ref[...] = prior + whole

    first_year = b * GROUP
    g = [gain[pl.ds(first_year + i, 1), :] for i in range(GROUP)]
    r = [back[pl.ds(first_year + i, 1), :] for i in range(GROUP)]
    w = [share[pl.ds(first_year + i, 1), :] for i in range(GROUP)]
    keep = []
    for i in range(GROUP):
        keep.append((1.0 - g[i]) * keep[-1] if i else 1.0 - g[i])
    hold = [jnp.ones_like(g[0])]
    for i in reversed(range(GROUP)):
        hold.insert(0, (1.0 - r[i]) * hold[0])
    block_keep, block_hold = [], []
    for other in range(n_blocks):
        years = range(other * GROUP, (other + 1) * GROUP)
        block_keep.append(functools.reduce(jnp.multiply, [1.0 - gain[y : y + 1, :] for y in years]))
        block_hold.append(functools.reduce(jnp.multiply, [1.0 - back[y : y + 1, :] for y in years]))
    into = []
    for other in range(n_blocks):
        fore = jnp.where(other < b, 1.0, 0.0)
        for between in range(other + 1, n_blocks):
            fore = fore * jnp.where(between < b, block_keep[between], 1.0)
        hind = jnp.where(other > b, 1.0, 0.0)
        for between in range(other):
            hind = hind * jnp.where(between > b, block_hold[between], 1.0)
        into.append((fore, hind))

    def mid_copy(c, off, other, source):
        which = jnp.where(other > b, 0, 1)
        return send(mid_out.at[c, which], mid_in.at[c, source], mid_send.at[c, off], mid_recv.at[c, source], other_id(other))

    for c in range(CHUNKS):
        years_in[c, m] = pseudo[word_rows(m, c), :]
        mid_in[c, b] = jnp.zeros((width, K), jnp.float32)
        for off, mate in mates:
            in_copy(c, mate, mate).wait_recv()
        ahead = g[0] * years_in[c, 0]
        local[c, 0] = w[0] * ahead
        for i in range(1, GROUP):
            ahead = g[i] * years_in[c, i] + (1.0 - g[i]) * ahead
            local[c, i] = w[i] * ahead
        mid_out[c, 0] = ahead
        behind = r[GROUP - 1] * years_in[c, GROUP - 1]
        for i in reversed(range(GROUP - 1)):
            local[c, i] += (1.0 - w[i]) * behind
            behind = r[i] * years_in[c, i] + (1.0 - r[i]) * behind
        mid_out[c, 1] = behind
        for off, other in others:
            mid_copy(c, off, other, b).start()

    def out_copy(c, mate, source):
        return send(
            years_out.at[c, mate], out_ref.at[word_rows(source, c), :], out_send.at[c, mate], out_recv.at[c, source], mate_id(mate)
        )

    for c in range(CHUNKS):
        for off, other in others:
            mid_copy(c, off, other, other).wait_recv()
        ahead, behind = 0.0, 0.0
        for other in range(n_blocks):
            value = mid_in[c, other]
            ahead = ahead + into[other][0] * value
            behind = behind + into[other][1] * value
        for i in range(GROUP):
            years_out[c, i] = local[c, i] + (w[i] * keep[i]) * ahead + ((1.0 - w[i]) * hold[i + 1]) * behind
        for off, mate in mates:
            out_copy(c, mate, m).start()
        out_ref[word_rows(m, c), :] = years_out[c, m]

    for c in range(CHUNKS):
        for off, mate in mates:
            out_copy(c, mate, mate).wait_recv()
    for off, peer in peers:
        msg_copy(off, peer, me).wait_send()
        for sweep in range(EITERS - 1):
            sum_copy(sweep, off, peer, me).wait_send()
        end_copy(off, peer, me).wait_send()
    for c in range(CHUNKS):
        for off, mate in mates:
            in_copy(c, mate, m).wait_send()
            out_copy(c, mate, m).wait_send()
        for off, other in others:
            mid_copy(c, off, other, b).wait_send()


def vmem():
    return pl.BlockSpec(memory_space=pltpu.VMEM)


def solution(mesh):
    n_tm, n_doc = mesh.shape["tm"], mesh.shape["doc"]

    def body(beta, word_ids, word_counts, block_slot, topic_prior, drift_var, obs_precision):
        local_beta, ids, cnt = beta[0], word_ids[0], word_counts[0]
        own, dpd = local_beta.shape[0], ids.shape[0]
        held = dpd * 128
        width = own // GROUP // CHUNKS
        n_blocks = n_tm // GROUP
        f32, bf16 = jnp.float32, jnp.bfloat16
        dma = pltpu.SemaphoreType.DMA
        smoothed, doc_topics = pl.pallas_call(
            functools.partial(kernel, n_tm, n_doc),
            out_shape=(jax.ShapeDtypeStruct((own, K), f32), jax.ShapeDtypeStruct((dpd, K), f32)),
            in_specs=[vmem(), vmem(), vmem(), pl.BlockSpec(memory_space=pltpu.SMEM), vmem(), vmem(), vmem()],
            out_specs=(vmem(), vmem()),
            scratch_shapes=[
                pltpu.VMEM((16, K), f32),
                pltpu.VMEM((n_doc, 16, K), f32),
                pltpu.VMEM((own // FOLD, FOLD * K), bf16),
                pltpu.VMEM((n_doc * held, K), f32),
                pltpu.VMEM((n_doc * held, K), f32),
                pltpu.VMEM((n_doc * held, K), f32),
                pltpu.VMEM((n_doc * held, FOLD * K), bf16),
                pltpu.VMEM((n_doc * dpd, K), f32),
                pltpu.VMEM((EITERS - 1, n_doc * dpd, K), f32),
                pltpu.VMEM((EITERS - 1, n_doc, n_doc * dpd, K), f32),
                pltpu.VMEM((n_doc, dpd, K), f32),
                pltpu.VMEM((n_doc, dpd, K), f32),
                pltpu.VMEM((n_tm, K), f32),
                pltpu.VMEM((n_tm, K), f32),
                pltpu.VMEM((n_tm, K), f32),
                pltpu.VMEM((own, K), f32),
                pltpu.VMEM((CHUNKS, GROUP, width, K), f32),
                pltpu.VMEM((CHUNKS, GROUP, width, K), f32),
                pltpu.VMEM((CHUNKS, 2, width, K), f32),
                pltpu.VMEM((CHUNKS, n_blocks, width, K), f32),
                pltpu.VMEM((CHUNKS, GROUP, width, K), f32),
                dma((n_doc,)),
                dma((n_doc,)),
                dma((EITERS - 1, n_doc)),
                dma((EITERS - 1, n_doc)),
                dma((n_doc,)),
                dma((n_doc,)),
                dma((CHUNKS, GROUP)),
                dma((CHUNKS, GROUP)),
                dma((CHUNKS, n_blocks)),
                dma((CHUNKS, n_blocks)),
                dma((CHUNKS, GROUP)),
                dma((CHUNKS, GROUP)),
            ],
            compiler_params=pltpu.CompilerParams(
                collective_id=0, has_side_effects=True, vmem_limit_bytes=48 * 1024 * 1024
            ),
            name="topics",
        )(local_beta, ids, cnt, block_slot, topic_prior[None], obs_precision, drift_var[None])
        return (smoothed[None], doc_topics[None])

    in_specs = (P("tm", "doc", None), P("tm", "doc", None), P("tm", "doc", None), P(), P(), P(), P())
    out_specs = (P("tm", "doc", None), P("tm", "doc", None))
    return jax.shard_map(body, mesh=mesh, in_specs=in_specs, out_specs=out_specs, check_vma=False)
```

```python
import functools
import math

import jax
import jax.numpy as jnp
from jax import lax
from jax.experimental import pallas as pl
from jax.experimental.pallas import tpu as pltpu
from jax.sharding import PartitionSpec as P

K = 128
BLOCK = 128
EITERS = 4
GROUP = 8
FOLD = 4
CHUNKS = 2
INIT_VAR = 4.0
MESH = pl.DeviceIdType.MESH


def exp_digamma(x):
    u = x * (x + 5.0)
    steps = (2.0 * x + 5.0) * ((3.0 * u + 20.0) * u + 24.0) / (u * (u + 4.0) * (u + 6.0))
    y = x + 6.0
    inv = 1.0 / y
    inv2 = inv * inv
    series = inv * 0.5 + inv2 * (1.0 / 12.0 - inv2 * (1.0 / 120.0 - inv2 * (1.0 / 252.0 - inv2 * (1.0 / 240.0))))
    return y * jnp.exp(-(series + steps))


FLOOR = 2.0**-10
LIMIT = 300.0
STEPS = 32766.0 / math.log2(1.0 + LIMIT / FLOOR)


def encode(value):
    size = jnp.log2(1.0 + jnp.abs(value) * (1.0 / FLOOR)) * STEPS + 0.5
    code = size.astype(jnp.int32)
    return jnp.where(value < 0.0, -code, code).astype(jnp.int16)


def decode(code):
    code = code.astype(jnp.float32)
    size = jnp.exp2(jnp.abs(code) * (1.0 / STEPS)) * FLOOR - FLOOR
    return jnp.where(code < 0.0, -size, size)


def send(src, dst, send_sem, recv_sem, where):
    return pltpu.make_async_remote_copy(
        src_ref=src, dst_ref=dst, send_sem=send_sem, recv_sem=recv_sem, device_id=where, device_id_type=MESH
    )


def far_first(count):
    return sorted(range(1, count), key=lambda off: abs(off - count // 2) + 2 * (1 - off % 2))


def kernel(
    n_tm,
    n_doc,
    beta_hbm,
    ids_hbm,
    cnt_hbm,
    slot_hbm,
    prior_hbm,
    prec_hbm,
    drift_hbm,
    out_ref,
    topics_ref,
    beta_ref,
    ids_ref,
    cnt_ref,
    slot_ref,
    prior_ref,
    prec_ref,
    drift_ref,
    load_sem,
    msg,
    land,
    table,
    expo,
    scale,
    quarter,
    weighted,
    alpha,
    part,
    sums,
    end_part,
    end_sums,
    gain,
    back,
    share,
    pseudo,
    years_in,
    local,
    mid_out,
    mid_in,
    years_out,
    coded,
    msg_send,
    msg_recv,
    sum_send,
    sum_recv,
    end_send,
    end_recv,
    in_send,
    in_recv,
    mid_send,
    mid_recv,
    out_send,
    out_recv,
):
    me = lax.axis_index("doc")
    t = lax.axis_index("tm")
    n_blocks = n_tm // GROUP
    b = t // GROUP
    m = lax.rem(t, GROUP)
    own = beta_ref.shape[0]
    dpd = ids_ref.shape[0]
    held = dpd * 128
    span = own // GROUP
    width = span // CHUNKS

    peers = [(off, lax.rem(me + off, n_doc)) for off in far_first(n_doc)]
    mates = [(off, lax.rem(m + off, GROUP)) for off in range(1, GROUP)]
    others = [(off, lax.rem(b + off, n_blocks)) for off in range(1, n_blocks)]

    def mate_id(mate):
        return {"tm": b * GROUP + mate}

    def other_id(other):
        return {"tm": other * GROUP + m}

    barrier = pltpu.get_barrier_semaphore()
    for _, peer in peers:
        pl.semaphore_signal(barrier, inc=1, device_id={"doc": peer}, device_id_type=MESH)
    for _, mate in mates:
        pl.semaphore_signal(barrier, inc=1, device_id=mate_id(mate), device_id_type=MESH)
    for _, other in others:
        pl.semaphore_signal(barrier, inc=1, device_id=other_id(other), device_id_type=MESH)

    loads = [
        pltpu.make_async_copy(source, held_here, load_sem.at[k])
        for k, (source, held_here) in enumerate(
            [
                (ids_hbm, ids_ref),
                (slot_hbm, slot_ref),
                (cnt_hbm, cnt_ref),
                (beta_hbm, beta_ref),
                (prec_hbm, prec_ref),
                (drift_hbm, drift_ref),
                (prior_hbm, prior_ref),
            ]
        )
    ]
    for load in loads:
        load.start()
    for load in loads:
        load.wait()

    ids = ids_ref[...]
    block_of = lax.shift_right_logical(ids, 7)
    inside = jnp.bitwise_and(ids, 127)
    place = jnp.zeros_like(ids)
    for k in range(slot_ref.shape[0]):
        place = jnp.where(block_of == k, slot_ref[k], place)
    columns = (place * BLOCK + inside).astype(jnp.float32)
    beta = beta_ref[...]
    peak = jnp.max(beta, axis=0, keepdims=True)
    total = jnp.sum(jnp.exp(beta - peak), axis=0, keepdims=True)
    msg[...] = jnp.zeros_like(msg)
    msg[0:dpd, :] = columns
    msg[dpd : dpd + 1, :] = peak
    msg[dpd + 1 : dpd + 2, :] = total
    msg[8 : 8 + dpd, :] = cnt_ref[...].astype(jnp.float32)
    land[me] = msg[...]

    pl.semaphore_wait(barrier, len(peers) + len(mates) + len(others))

    def msg_copy(off, peer, source):
        return send(msg, land.at[source], msg_send.at[off], msg_recv.at[source], {"doc": peer})

    for off, peer in peers:
        msg_copy(off, peer, me).start()

    drift = drift_ref[...]
    var = jnp.full_like(drift, INIT_VAR)
    filt = []
    for k in range(n_tm):
        precision = prec_ref[k : k + 1, :]
        inverse = 1.0 / (1.0 + var * precision)
        gain[k : k + 1, :] = var * precision * inverse
        filt.append(var * inverse)
        var = filt[k] + drift
    info = jnp.zeros_like(drift)
    for k in reversed(range(n_tm)):
        share[k : k + 1, :] = 1.0 / (1.0 + filt[k] * info)
        precision = prec_ref[k : k + 1, :]
        merged = info + precision
        back[k : k + 1, :] = precision / merged
        info = merged / (1.0 + drift * merged)
    prior = prior_ref[...]

    for off, peer in peers:
        msg_copy(off, peer, peer).wait_recv()

    peaks = [land[s, dpd : dpd + 1, :] for s in range(n_doc)]
    peak = functools.reduce(jnp.maximum, peaks)
    total = sum(land[s, dpd + 1 : dpd + 2, :] * jnp.exp(peaks[s] - peak) for s in range(n_doc))
    normalizer = peak + jnp.log(total)
    fold = own // FOLD
    for f in range(FOLD):
        table[:, f * K : (f + 1) * K] = (beta_ref[f * fold : (f + 1) * fold, :] - normalizer).astype(jnp.bfloat16)

    base = (me * own).astype(jnp.float32)
    lanes = lax.broadcasted_iota(jnp.int32, (128, 128), 1).astype(jnp.float32)

    for s in range(n_doc):
        start = jnp.sum(land[s, 8 : 8 + dpd, :], axis=1, keepdims=True) / K
        alpha[s * dpd : (s + 1) * dpd, :] = jnp.broadcast_to(start, (dpd, K))
    alpha[...] = exp_digamma(prior + alpha[...])

    def look_up(s, _):
        marks, parts = [], []
        for i in range(dpd):
            both = land[s, pl.ds(i, 1), :] * 16.0 + land[s, pl.ds(8 + i, 1), :]
            both = jnp.transpose(jnp.broadcast_to(both, (128, 128)))
            col = jnp.floor(both * (1.0 / 16.0))
            cnt = both - 16.0 * col
            col = col - base
            part_of = jnp.floor(col * (1.0 / fold))
            rest = col - float(fold) * part_of
            parts.append(part_of)
            at = pl.ds(pl.multiple_of((s * dpd + i) * 128, 128), 128)
            scale[at, :] = jnp.where((part_of >= 0.0) & (part_of < float(FOLD)), cnt, 0.0)
            quarter[at, :] = part_of
            marks.append(
                jnp.concatenate(
                    [(rest == lanes + float(128 * j)).astype(jnp.bfloat16) for j in range(fold // 128)], axis=1
                )
            )
        wide = jnp.dot(jnp.concatenate(marks, axis=0), table[...], preferred_element_type=jnp.float32)
        part_of = jnp.concatenate(parts, axis=0)
        looked = wide[:, 0:K]
        for f in range(1, FOLD):
            looked = jnp.where(part_of == float(f), wide[:, f * K : (f + 1) * K], looked)
        at = pl.ds(pl.multiple_of(s * held, held), held)
        expo[at, :] = jnp.exp(looked - jnp.max(looked, axis=1, keepdims=True))
        return 0

    lax.fori_loop(0, n_doc, look_up, 0, unroll=2)

    def sum_copy(sweep, off, peer, source):
        return send(part.at[sweep], sums.at[sweep, source], sum_send.at[sweep, off], sum_recv.at[sweep, source], {"doc": peer})

    def end_copy(off, peer, source):
        return send(end_part.at[peer], end_sums.at[source], end_send.at[off], end_recv.at[source], {"doc": peer})

    for sweep in range(EITERS):
        last = sweep == EITERS - 1

        def e_step(s, _, last=last, sweep=sweep):
            for i in range(dpd):
                row = s * dpd + i
                at = pl.ds(pl.multiple_of(row * 128, 128), 128)
                scaled = expo[at, :] * alpha[pl.ds(row, 1), :]
                scaled = scaled * (scale[at, :] * (1.0 / jnp.sum(scaled, axis=1, keepdims=True)))
                if last:
                    end_part[s, i : i + 1, :] = jnp.sum(scaled, axis=0, keepdims=True)
                    for f in range(FOLD):
                        weighted[at, f * K : (f + 1) * K] = jnp.where(quarter[at, :] == float(f), scaled, 0.0).astype(
                            jnp.bfloat16
                        )
                else:
                    part[sweep, pl.ds(row, 1), :] = jnp.sum(scaled, axis=0, keepdims=True)
            return 0

        lax.fori_loop(0, n_doc, e_step, 0, unroll=2)
        if not last:
            for off, peer in peers:
                sum_copy(sweep, off, peer, me).start()
            sums[sweep, me] = part[sweep]
            for off, peer in peers:
                sum_copy(sweep, off, peer, peer).wait_recv()
            whole = sums[sweep, 0]
            for s in range(1, n_doc):
                whole = whole + sums[sweep, s]
            alpha[...] = exp_digamma(prior + whole)
        else:
            for off, peer in peers:
                end_copy(off, peer, me).start()
            end_sums[me] = end_part[me]

    def word_rows(mate, c):
        return pl.ds(pl.multiple_of(mate * span + c * width, width), width)

    def in_copy(c, mate, source):
        return send(
            pseudo.at[word_rows(mate, c), :], years_in.at[c, source], in_send.at[c, mate], in_recv.at[c, source], mate_id(mate)
        )

    spans = fold // span
    rests = []
    for s in range(n_doc):
        col = land[s, 0:dpd, :] - base
        rests.append(col - float(fold) * jnp.floor(col * (1.0 / fold)))
    words = lax.broadcasted_iota(jnp.int32, (width, 128), 0).astype(jnp.float32)
    for c in range(CHUNKS):
        marks = []
        for s in range(n_doc):
            for i in range(dpd):
                marks.append(
                    jnp.concatenate(
                        [
                            (words + float(h * span + c * width) == rests[s][i : i + 1, :]).astype(jnp.bfloat16)
                            for h in range(spans)
                        ],
                        axis=0,
                    )
                )
        counts = jnp.dot(jnp.concatenate(marks, axis=1), weighted[...], preferred_element_type=jnp.float32)
        for h in range(spans):
            for f in range(FOLD):
                mate = f * spans + h
                first = mate * span + c * width
                whole = counts[h * width : (h + 1) * width, f * K : (f + 1) * K]
                pseudo[first : first + width, :] = encode(beta_ref[first : first + width, :] + jnp.log1p(whole))

                @pl.when(mate != m)
                def _(mate=mate, c=c):
                    in_copy(c, mate, m).start()

    for off, peer in peers:
        end_copy(off, peer, peer).wait_recv()
    whole = end_sums[0]
    for s in range(1, n_doc):
        whole = whole + end_sums[s]
    topics_ref[...] = prior + whole

    first_year = b * GROUP
    g = [gain[pl.ds(first_year + i, 1), :] for i in range(GROUP)]
    r = [back[pl.ds(first_year + i, 1), :] for i in range(GROUP)]
    w = [share[pl.ds(first_year + i, 1), :] for i in range(GROUP)]
    keep = []
    for i in range(GROUP):
        keep.append((1.0 - g[i]) * keep[-1] if i else 1.0 - g[i])
    hold = [jnp.ones_like(g[0])]
    for i in reversed(range(GROUP)):
        hold.insert(0, (1.0 - r[i]) * hold[0])
    block_keep, block_hold = [], []
    for other in range(n_blocks):
        years = range(other * GROUP, (other + 1) * GROUP)
        block_keep.append(functools.reduce(jnp.multiply, [1.0 - gain[y : y + 1, :] for y in years]))
        block_hold.append(functools.reduce(jnp.multiply, [1.0 - back[y : y + 1, :] for y in years]))
    into = []
    for other in range(n_blocks):
        fore = jnp.where(other < b, 1.0, 0.0)
        for between in range(other + 1, n_blocks):
            fore = fore * jnp.where(between < b, block_keep[between], 1.0)
        hind = jnp.where(other > b, 1.0, 0.0)
        for between in range(other):
            hind = hind * jnp.where(between > b, block_hold[between], 1.0)
        into.append((fore, hind))

    def mid_copy(c, off, other, source):
        which = jnp.where(other > b, 0, 1)
        return send(mid_out.at[c, which], mid_in.at[c, source], mid_send.at[c, off], mid_recv.at[c, source], other_id(other))

    for c in range(CHUNKS):
        years_in[c, m] = pseudo[word_rows(m, c), :]
        mid_in[c, b] = jnp.zeros((width, K), jnp.int16)
        for off, mate in mates:
            in_copy(c, mate, mate).wait_recv()
        values = [decode(years_in[c, i]) for i in range(GROUP)]
        ahead = g[0] * values[0]
        local[c, 0] = w[0] * ahead
        for i in range(1, GROUP):
            ahead = g[i] * values[i] + (1.0 - g[i]) * ahead
            local[c, i] = w[i] * ahead
        mid_out[c, 0] = encode(ahead)
        behind = r[GROUP - 1] * values[GROUP - 1]
        for i in reversed(range(GROUP - 1)):
            local[c, i] += (1.0 - w[i]) * behind
            behind = r[i] * values[i] + (1.0 - r[i]) * behind
        mid_out[c, 1] = encode(behind)
        for off, other in others:
            mid_copy(c, off, other, b).start()

    def out_copy(c, mate, source):
        return send(
            years_out.at[c, mate], coded.at[word_rows(source, c), :], out_send.at[c, mate], out_recv.at[c, source], mate_id(mate)
        )

    for c in range(CHUNKS):
        for off, other in others:
            mid_copy(c, off, other, other).wait_recv()
        ahead, behind = 0.0, 0.0
        for other in range(n_blocks):
            value = decode(mid_in[c, other])
            ahead = ahead + into[other][0] * value
            behind = behind + into[other][1] * value
        for i in range(GROUP):
            years_out[c, i] = encode(local[c, i] + (w[i] * keep[i]) * ahead + ((1.0 - w[i]) * hold[i + 1]) * behind)
        for off, mate in mates:
            out_copy(c, mate, m).start()
        out_ref[word_rows(m, c), :] = decode(years_out[c, m])

    for c in range(CHUNKS):
        for off, mate in mates:
            out_copy(c, mate, mate).wait_recv()
            out_ref[word_rows(mate, c), :] = decode(coded[word_rows(mate, c), :])
    for off, peer in peers:
        msg_copy(off, peer, me).wait_send()
        for sweep in range(EITERS - 1):
            sum_copy(sweep, off, peer, me).wait_send()
        end_copy(off, peer, me).wait_send()
    for c in range(CHUNKS):
        for off, mate in mates:
            in_copy(c, mate, m).wait_send()
            out_copy(c, mate, m).wait_send()
        for off, other in others:
            mid_copy(c, off, other, b).wait_send()


def vmem():
    return pl.BlockSpec(memory_space=pltpu.VMEM)


def solution(mesh):
    n_tm, n_doc = mesh.shape["tm"], mesh.shape["doc"]

    def body(beta, word_ids, word_counts, block_slot, topic_prior, drift_var, obs_precision):
        local_beta, ids, cnt = beta[0], word_ids[0], word_counts[0]
        own, dpd = local_beta.shape[0], ids.shape[0]
        held = dpd * 128
        width = own // GROUP // CHUNKS
        n_blocks = n_tm // GROUP
        f32, bf16, link = jnp.float32, jnp.bfloat16, jnp.int16
        dma = pltpu.SemaphoreType.DMA
        smoothed, doc_topics = pl.pallas_call(
            functools.partial(kernel, n_tm, n_doc),
            out_shape=(jax.ShapeDtypeStruct((own, K), f32), jax.ShapeDtypeStruct((dpd, K), f32)),
            in_specs=[pl.BlockSpec(memory_space=pltpu.HBM)] * 7,
            out_specs=(vmem(), vmem()),
            scratch_shapes=[
                pltpu.VMEM((own, K), f32),
                pltpu.VMEM((dpd, 128), jnp.int32),
                pltpu.VMEM((dpd, 128), jnp.int32),
                pltpu.SMEM(block_slot.shape, jnp.int32),
                pltpu.VMEM((1, K), f32),
                pltpu.VMEM((n_tm, K), f32),
                pltpu.VMEM((1, K), f32),
                dma((7,)),
                pltpu.VMEM((16, K), f32),
                pltpu.VMEM((n_doc, 16, K), f32),
                pltpu.VMEM((own // FOLD, FOLD * K), bf16),
                pltpu.VMEM((n_doc * held, K), f32),
                pltpu.VMEM((n_doc * held, K), f32),
                pltpu.VMEM((n_doc * held, K), f32),
                pltpu.VMEM((n_doc * held, FOLD * K), bf16),
                pltpu.VMEM((n_doc * dpd, K), f32),
                pltpu.VMEM((EITERS - 1, n_doc * dpd, K), f32),
                pltpu.VMEM((EITERS - 1, n_doc, n_doc * dpd, K), f32),
                pltpu.VMEM((n_doc, dpd, K), f32),
                pltpu.VMEM((n_doc, dpd, K), f32),
                pltpu.VMEM((n_tm, K), f32),
                pltpu.VMEM((n_tm, K), f32),
                pltpu.VMEM((n_tm, K), f32),
                pltpu.VMEM((own, K), link),
                pltpu.VMEM((CHUNKS, GROUP, width, K), link),
                pltpu.VMEM((CHUNKS, GROUP, width, K), f32),
                pltpu.VMEM((CHUNKS, 2, width, K), link),
                pltpu.VMEM((CHUNKS, n_blocks, width, K), link),
                pltpu.VMEM((CHUNKS, GROUP, width, K), link),
                pltpu.VMEM((own, K), link),
                dma((n_doc,)),
                dma((n_doc,)),
                dma((EITERS - 1, n_doc)),
                dma((EITERS - 1, n_doc)),
                dma((n_doc,)),
                dma((n_doc,)),
                dma((CHUNKS, GROUP)),
                dma((CHUNKS, GROUP)),
                dma((CHUNKS, n_blocks)),
                dma((CHUNKS, n_blocks)),
                dma((CHUNKS, GROUP)),
                dma((CHUNKS, GROUP)),
            ],
            compiler_params=pltpu.CompilerParams(
                collective_id=0, has_side_effects=True, vmem_limit_bytes=48 * 1024 * 1024
            ),
            name="topics",
        )(*[
            pltpu.with_memory_space_constraint(a, pltpu.HBM)
            for a in (local_beta, ids, cnt, block_slot, topic_prior[None], obs_precision, drift_var[None])
        ])
        return (smoothed[None], doc_topics[None])

    in_specs = (P("tm", "doc", None), P("tm", "doc", None), P("tm", "doc", None), P(), P(), P(), P())
    out_specs = (P("tm", "doc", None), P("tm", "doc", None))
    return jax.shard_map(body, mesh=mesh, in_specs=in_specs, out_specs=out_specs, check_vma=False)
```

```python
import functools
import math

import jax
import jax.numpy as jnp
from jax import lax
from jax.experimental import pallas as pl
from jax.experimental.pallas import tpu as pltpu
from jax.sharding import PartitionSpec as P

K = 128
BLOCK = 128
EITERS = 4
GROUP = 8
FOLD = 4
CHUNKS = 2
INIT_VAR = 4.0
MESH = pl.DeviceIdType.MESH


def exp_digamma(x):
    u = x * (x + 5.0)
    steps = (2.0 * x + 5.0) * ((3.0 * u + 20.0) * u + 24.0) / (u * (u + 4.0) * (u + 6.0))
    y = x + 6.0
    inv = 1.0 / y
    inv2 = inv * inv
    series = inv * 0.5 + inv2 * (1.0 / 12.0 - inv2 * (1.0 / 120.0 - inv2 * (1.0 / 252.0 - inv2 * (1.0 / 240.0))))
    return y * jnp.exp(-(series + steps))


FLOOR = 2.0**-10
LIMIT = 300.0
STEPS = 32766.0 / math.log2(1.0 + LIMIT / FLOOR)


def encode(value):
    size = jnp.log2(1.0 + jnp.abs(value) * (1.0 / FLOOR)) * STEPS + 0.5
    code = size.astype(jnp.int32)
    return jnp.where(value < 0.0, -code, code).astype(jnp.int16)


def decode(code):
    code = code.astype(jnp.float32)
    size = jnp.exp2(jnp.abs(code) * (1.0 / STEPS)) * FLOOR - FLOOR
    return jnp.where(code < 0.0, -size, size)


def send(src, dst, send_sem, recv_sem, where):
    return pltpu.make_async_remote_copy(
        src_ref=src, dst_ref=dst, send_sem=send_sem, recv_sem=recv_sem, device_id=where, device_id_type=MESH
    )


def far_first(count):
    return sorted(range(1, count), key=lambda off: abs(off - count // 2) + 2 * (1 - off % 2))


def kernel(
    n_tm,
    n_doc,
    beta_hbm,
    ids_hbm,
    cnt_hbm,
    slot_hbm,
    prior_hbm,
    prec_hbm,
    drift_hbm,
    out_ref,
    topics_ref,
    beta_ref,
    ids_ref,
    cnt_ref,
    slot_ref,
    prior_ref,
    prec_ref,
    drift_ref,
    load_sem,
    msg,
    land,
    table,
    expo,
    scale,
    quarter,
    weighted,
    alpha,
    part,
    sums,
    end_part,
    end_sums,
    gain,
    back,
    share,
    pseudo,
    years_in,
    local,
    mid_out,
    mid_in,
    years_out,
    coded,
    msg_send,
    msg_recv,
    sum_send,
    sum_recv,
    end_send,
    end_recv,
    in_send,
    in_recv,
    mid_send,
    mid_recv,
    out_send,
    out_recv,
):
    me = lax.axis_index("doc")
    t = lax.axis_index("tm")
    n_blocks = n_tm // GROUP
    b = t // GROUP
    m = lax.rem(t, GROUP)
    own = beta_ref.shape[0]
    dpd = ids_ref.shape[0]
    held = dpd * 128
    span = own // GROUP
    width = span // CHUNKS

    peers = [(off, lax.rem(me + off, n_doc)) for off in far_first(n_doc)]
    mates = [(off, lax.rem(m + off, GROUP)) for off in range(1, GROUP)]
    others = [(off, lax.rem(b + off, n_blocks)) for off in sorted(range(1, n_blocks), key=lambda off: abs(off - n_blocks // 2))]

    def mate_id(mate):
        return {"tm": b * GROUP + mate}

    def other_id(other):
        return {"tm": other * GROUP + m}

    barrier = pltpu.get_barrier_semaphore()
    for _, peer in peers:
        pl.semaphore_signal(barrier, inc=1, device_id={"doc": peer}, device_id_type=MESH)
    for _, other in others:
        pl.semaphore_signal(barrier, inc=1, device_id=other_id(other), device_id_type=MESH)
    for _, mate in mates:
        pl.semaphore_signal(barrier, inc=1, device_id=mate_id(mate), device_id_type=MESH)

    loads = [
        pltpu.make_async_copy(source, held_here, load_sem.at[k])
        for k, (source, held_here) in enumerate(
            [
                (ids_hbm, ids_ref),
                (slot_hbm, slot_ref),
                (cnt_hbm, cnt_ref),
                (beta_hbm, beta_ref),
                (prec_hbm, prec_ref),
                (drift_hbm, drift_ref),
                (prior_hbm, prior_ref),
            ]
        )
    ]
    for load in loads:
        load.start()
    for load in loads:
        load.wait()

    ids = ids_ref[...]
    block_of = lax.shift_right_logical(ids, 7)
    inside = jnp.bitwise_and(ids, 127)
    place = jnp.zeros_like(ids)
    for k in range(slot_ref.shape[0]):
        place = jnp.where(block_of == k, slot_ref[k], place)
    columns = (place * BLOCK + inside).astype(jnp.float32)
    beta = beta_ref[...]
    peak = jnp.max(beta, axis=0, keepdims=True)
    total = jnp.sum(jnp.exp(beta - peak), axis=0, keepdims=True)
    msg[...] = jnp.zeros_like(msg)
    msg[0:dpd, :] = columns
    msg[dpd : dpd + 1, :] = peak
    msg[dpd + 1 : dpd + 2, :] = total
    msg[8 : 8 + dpd, :] = cnt_ref[...].astype(jnp.float32)
    land[me] = msg[...]

    pl.semaphore_wait(barrier, len(peers) + len(mates) + len(others))

    def msg_copy(off, peer, source):
        return send(msg, land.at[source], msg_send.at[off], msg_recv.at[source], {"doc": peer})

    for off, peer in peers:
        msg_copy(off, peer, me).start()

    drift = drift_ref[...]
    var = jnp.full_like(drift, INIT_VAR)
    filt = []
    for k in range(n_tm):
        precision = prec_ref[k : k + 1, :]
        inverse = 1.0 / (1.0 + var * precision)
        gain[k : k + 1, :] = var * precision * inverse
        filt.append(var * inverse)
        var = filt[k] + drift
    info = jnp.zeros_like(drift)
    for k in reversed(range(n_tm)):
        share[k : k + 1, :] = 1.0 / (1.0 + filt[k] * info)
        precision = prec_ref[k : k + 1, :]
        merged = info + precision
        back[k : k + 1, :] = precision / merged
        info = merged / (1.0 + drift * merged)
    prior = prior_ref[...]

    for off, peer in peers:
        msg_copy(off, peer, peer).wait_recv()

    peaks = [land[s, dpd : dpd + 1, :] for s in range(n_doc)]
    peak = functools.reduce(jnp.maximum, peaks)
    total = sum(land[s, dpd + 1 : dpd + 2, :] * jnp.exp(peaks[s] - peak) for s in range(n_doc))
    normalizer = peak + jnp.log(total)
    fold = own // FOLD
    for f in range(FOLD):
        table[:, f * K : (f + 1) * K] = (beta_ref[f * fold : (f + 1) * fold, :] - normalizer).astype(jnp.bfloat16)

    base = (me * own).astype(jnp.float32)
    lanes = lax.broadcasted_iota(jnp.int32, (128, 128), 1).astype(jnp.float32)

    for s in range(n_doc):
        start = jnp.sum(land[s, 8 : 8 + dpd, :], axis=1, keepdims=True) / K
        row = (s % (n_doc // 2)) * dpd
        alpha[s // (n_doc // 2), row : row + dpd, :] = jnp.broadcast_to(start, (dpd, K))
    alpha[...] = exp_digamma(prior + alpha[...])

    def look_up(s, _):
        marks, parts = [], []
        for i in range(dpd):
            both = land[s, pl.ds(i, 1), :] * 16.0 + land[s, pl.ds(8 + i, 1), :]
            both = jnp.transpose(jnp.broadcast_to(both, (128, 128)))
            col = jnp.floor(both * (1.0 / 16.0))
            cnt = both - 16.0 * col
            col = col - base
            part_of = jnp.floor(col * (1.0 / fold))
            rest = col - float(fold) * part_of
            parts.append(part_of)
            at = pl.ds(pl.multiple_of((s * dpd + i) * 128, 128), 128)
            scale[at, :] = jnp.where((part_of >= 0.0) & (part_of < float(FOLD)), cnt, 0.0)
            quarter[at, :] = part_of
            marks.append(
                jnp.concatenate(
                    [(rest == lanes + float(128 * j)).astype(jnp.bfloat16) for j in range(fold // 128)], axis=1
                )
            )
        wide = jnp.dot(jnp.concatenate(marks, axis=0), table[...], preferred_element_type=jnp.float32)
        part_of = jnp.concatenate(parts, axis=0)
        looked = wide[:, 0:K]
        for f in range(1, FOLD):
            looked = jnp.where(part_of == float(f), wide[:, f * K : (f + 1) * K], looked)
        at = pl.ds(pl.multiple_of(s * held, held), held)
        expo[at, :] = jnp.exp(looked - jnp.max(looked, axis=1, keepdims=True))
        return 0

    lax.fori_loop(0, n_doc, look_up, 0, unroll=n_doc)

    def sum_copy(sweep, half, off, peer, source):
        turn = 2 * sweep + half
        return send(
            part.at[sweep, half], sums.at[sweep, source, half], sum_send.at[turn, off], sum_recv.at[turn, source], {"doc": peer}
        )

    def end_copy(off, peer, source):
        return send(end_part.at[peer], end_sums.at[source], end_send.at[off], end_recv.at[source], {"doc": peer})

    side = n_doc // 2
    for sweep in range(EITERS):
        last = sweep == EITERS - 1
        for half in range(2):
            if sweep:
                for off, peer in reversed(peers):
                    sum_copy(sweep - 1, half, off, peer, peer).wait_recv()
                whole = sums[sweep - 1, 0, half]
                for s in range(1, n_doc):
                    whole = whole + sums[sweep - 1, s, half]
                alpha[half] = exp_digamma(prior + whole)

            def e_step(s, _, last=last, sweep=sweep, half=half):
                for i in range(dpd):
                    row = s * dpd + i
                    at = pl.ds(pl.multiple_of((half * side * dpd + row) * 128, 128), 128)
                    scaled = expo[at, :] * alpha[half, pl.ds(row, 1), :]
                    scaled = scaled * (scale[at, :] * (1.0 / jnp.sum(scaled, axis=1, keepdims=True)))
                    if last:
                        end_part[half * side + s, i : i + 1, :] = jnp.sum(scaled, axis=0, keepdims=True)
                        for f in range(FOLD):
                            weighted[at, f * K : (f + 1) * K] = jnp.where(quarter[at, :] == float(f), scaled, 0.0).astype(
                                jnp.bfloat16
                            )
                    else:
                        part[sweep, half, pl.ds(row, 1), :] = jnp.sum(scaled, axis=0, keepdims=True)
                return 0

            lax.fori_loop(0, side, e_step, 0, unroll=side)
            if not last:
                for off, peer in peers:
                    sum_copy(sweep, half, off, peer, me).start()
                sums[sweep, me, half] = part[sweep, half]

    def word_rows(mate, c):
        return pl.ds(pl.multiple_of(mate * span + c * width, width), width)

    def in_copy(c, mate, source):
        return send(
            pseudo.at[word_rows(mate, c), :], years_in.at[c, source], in_send.at[c, mate], in_recv.at[c, source], mate_id(mate)
        )

    spans = fold // span
    rests = []
    for s in range(n_doc):
        col = land[s, 0:dpd, :] - base
        rests.append(col - float(fold) * jnp.floor(col * (1.0 / fold)))
    words = lax.broadcasted_iota(jnp.int32, (width, 128), 0).astype(jnp.float32)
    for c in range(CHUNKS):
        marks = []
        for s in range(n_doc):
            for i in range(dpd):
                marks.append(
                    jnp.concatenate(
                        [
                            (words + float(h * span + c * width) == rests[s][i : i + 1, :]).astype(jnp.bfloat16)
                            for h in range(spans)
                        ],
                        axis=0,
                    )
                )
        counts = jnp.dot(jnp.concatenate(marks, axis=1), weighted[...], preferred_element_type=jnp.float32)
        for h in range(spans):
            for f in range(FOLD):
                mate = f * spans + h
                first = mate * span + c * width
                whole = counts[h * width : (h + 1) * width, f * K : (f + 1) * K]
                pseudo[first : first + width, :] = encode(beta_ref[first : first + width, :] + jnp.log(1.0 + whole))

                @pl.when(mate != m)
                def _(mate=mate, c=c):
                    in_copy(c, mate, m).start()

    for off, peer in peers:
        end_copy(off, peer, me).start()
    end_sums[me] = end_part[me]

    first_year = b * GROUP
    g = [gain[pl.ds(first_year + i, 1), :] for i in range(GROUP)]
    r = [back[pl.ds(first_year + i, 1), :] for i in range(GROUP)]
    w = [share[pl.ds(first_year + i, 1), :] for i in range(GROUP)]
    keep = []
    for i in range(GROUP):
        keep.append((1.0 - g[i]) * keep[-1] if i else 1.0 - g[i])
    hold = [jnp.ones_like(g[0])]
    for i in reversed(range(GROUP)):
        hold.insert(0, (1.0 - r[i]) * hold[0])
    block_keep, block_hold = [], []
    for other in range(n_blocks):
        years = range(other * GROUP, (other + 1) * GROUP)
        block_keep.append(functools.reduce(jnp.multiply, [1.0 - gain[y : y + 1, :] for y in years]))
        block_hold.append(functools.reduce(jnp.multiply, [1.0 - back[y : y + 1, :] for y in years]))
    into = []
    for other in range(n_blocks):
        fore = jnp.where(other < b, 1.0, 0.0)
        for between in range(other + 1, n_blocks):
            fore = fore * jnp.where(between < b, block_keep[between], 1.0)
        hind = jnp.where(other > b, 1.0, 0.0)
        for between in range(other):
            hind = hind * jnp.where(between > b, block_hold[between], 1.0)
        into.append((fore, hind))

    def mid_copy(c, off, other, source):
        which = jnp.where(other > b, 0, 1)
        return send(mid_out.at[c, which], mid_in.at[c, source], mid_send.at[c, off], mid_recv.at[c, source], other_id(other))

    for off, peer in peers:
        msg_copy(off, peer, me).wait_send()
        for sweep in range(EITERS - 1):
            for half in range(2):
                sum_copy(sweep, half, off, peer, me).wait_send()

    for c in range(CHUNKS):
        years_in[c, m] = pseudo[word_rows(m, c), :]
        mid_in[c, b] = jnp.zeros((width, K), jnp.int16)
        for off, mate in mates:
            in_copy(c, mate, mate).wait_recv()
        values = [decode(years_in[c, i]) for i in range(GROUP)]
        ahead = g[0] * values[0]
        local[c, 0] = w[0] * ahead
        for i in range(1, GROUP):
            ahead = g[i] * values[i] + (1.0 - g[i]) * ahead
            local[c, i] = w[i] * ahead
        mid_out[c, 0] = encode(ahead)
        behind = r[GROUP - 1] * values[GROUP - 1]
        for i in reversed(range(GROUP - 1)):
            local[c, i] += (1.0 - w[i]) * behind
            behind = r[i] * values[i] + (1.0 - r[i]) * behind
        mid_out[c, 1] = encode(behind)
        for off, other in others:
            mid_copy(c, off, other, b).start()

    for off, peer in peers:
        end_copy(off, peer, peer).wait_recv()
    whole = end_sums[0]
    for s in range(1, n_doc):
        whole = whole + end_sums[s]
    topics_ref[...] = prior + whole

    for off, peer in peers:
        end_copy(off, peer, me).wait_send()
    for c in range(CHUNKS):
        for off, mate in mates:
            in_copy(c, mate, m).wait_send()

    def out_copy(c, mate, source):
        return send(
            years_out.at[c, mate], coded.at[word_rows(source, c), :], out_send.at[c, mate], out_recv.at[c, source], mate_id(mate)
        )

    for c in range(CHUNKS):
        for off, other in others:
            mid_copy(c, off, other, other).wait_recv()
        ahead, behind = 0.0, 0.0
        for other in range(n_blocks):
            value = decode(mid_in[c, other])
            ahead = ahead + into[other][0] * value
            behind = behind + into[other][1] * value
        for i in range(GROUP):
            years_out[c, i] = encode(local[c, i] + (w[i] * keep[i]) * ahead + ((1.0 - w[i]) * hold[i + 1]) * behind)
        for off, mate in mates:
            out_copy(c, mate, m).start()
        out_ref[word_rows(m, c), :] = decode(years_out[c, m])

    for c in range(CHUNKS):
        for off, other in others:
            mid_copy(c, off, other, b).wait_send()
    for c in range(CHUNKS):
        for off, mate in mates:
            out_copy(c, mate, mate).wait_recv()
            out_ref[word_rows(mate, c), :] = decode(coded[word_rows(mate, c), :])
    for c in range(CHUNKS):
        for off, mate in mates:
            out_copy(c, mate, m).wait_send()


def vmem():
    return pl.BlockSpec(memory_space=pltpu.VMEM)


def solution(mesh):
    n_tm, n_doc = mesh.shape["tm"], mesh.shape["doc"]

    def body(beta, word_ids, word_counts, block_slot, topic_prior, drift_var, obs_precision):
        local_beta, ids, cnt = beta[0], word_ids[0], word_counts[0]
        own, dpd = local_beta.shape[0], ids.shape[0]
        held = dpd * 128
        width = own // GROUP // CHUNKS
        n_blocks = n_tm // GROUP
        f32, bf16, link = jnp.float32, jnp.bfloat16, jnp.int16
        dma = pltpu.SemaphoreType.DMA
        smoothed, doc_topics = pl.pallas_call(
            functools.partial(kernel, n_tm, n_doc),
            out_shape=(jax.ShapeDtypeStruct((own, K), f32), jax.ShapeDtypeStruct((dpd, K), f32)),
            in_specs=[pl.BlockSpec(memory_space=pltpu.HBM)] * 7,
            out_specs=(vmem(), vmem()),
            scratch_shapes=[
                pltpu.VMEM((own, K), f32),
                pltpu.VMEM((dpd, 128), jnp.int32),
                pltpu.VMEM((dpd, 128), jnp.int32),
                pltpu.SMEM(block_slot.shape, jnp.int32),
                pltpu.VMEM((1, K), f32),
                pltpu.VMEM((n_tm, K), f32),
                pltpu.VMEM((1, K), f32),
                dma((7,)),
                pltpu.VMEM((16, K), f32),
                pltpu.VMEM((n_doc, 16, K), f32),
                pltpu.VMEM((own // FOLD, FOLD * K), bf16),
                pltpu.VMEM((n_doc * held, K), f32),
                pltpu.VMEM((n_doc * held, K), f32),
                pltpu.VMEM((n_doc * held, K), f32),
                pltpu.VMEM((n_doc * held, FOLD * K), bf16),
                pltpu.VMEM((2, n_doc // 2 * dpd, K), f32),
                pltpu.VMEM((EITERS - 1, 2, n_doc // 2 * dpd, K), f32),
                pltpu.VMEM((EITERS - 1, n_doc, 2, n_doc // 2 * dpd, K), f32),
                pltpu.VMEM((n_doc, dpd, K), f32),
                pltpu.VMEM((n_doc, dpd, K), f32),
                pltpu.VMEM((n_tm, K), f32),
                pltpu.VMEM((n_tm, K), f32),
                pltpu.VMEM((n_tm, K), f32),
                pltpu.VMEM((own, K), link),
                pltpu.VMEM((CHUNKS, GROUP, width, K), link),
                pltpu.VMEM((CHUNKS, GROUP, width, K), f32),
                pltpu.VMEM((CHUNKS, 2, width, K), link),
                pltpu.VMEM((CHUNKS, n_blocks, width, K), link),
                pltpu.VMEM((CHUNKS, GROUP, width, K), link),
                pltpu.VMEM((own, K), link),
                dma((n_doc,)),
                dma((n_doc,)),
                dma((2 * EITERS - 2, n_doc)),
                dma((2 * EITERS - 2, n_doc)),
                dma((n_doc,)),
                dma((n_doc,)),
                dma((CHUNKS, GROUP)),
                dma((CHUNKS, GROUP)),
                dma((CHUNKS, n_blocks)),
                dma((CHUNKS, n_blocks)),
                dma((CHUNKS, GROUP)),
                dma((CHUNKS, GROUP)),
            ],
            compiler_params=pltpu.CompilerParams(
                collective_id=0, has_side_effects=True, vmem_limit_bytes=48 * 1024 * 1024
            ),
            name="topics",
        )(*[
            pltpu.with_memory_space_constraint(a, pltpu.HBM)
            for a in (local_beta, ids, cnt, block_slot, topic_prior[None], obs_precision, drift_var[None])
        ])
        return (smoothed[None], doc_topics[None])

    in_specs = (P("tm", "doc", None), P("tm", "doc", None), P("tm", "doc", None), P(), P(), P(), P())
    out_specs = (P("tm", "doc", None), P("tm", "doc", None))
    return jax.shard_map(body, mesh=mesh, in_specs=in_specs, out_specs=out_specs, check_vma=False)
```

```python
import functools
import math

import jax
import jax.numpy as jnp
from jax import lax
from jax.experimental import pallas as pl
from jax.experimental.pallas import tpu as pltpu
from jax.sharding import PartitionSpec as P

K = 128
BLOCK = 128
EITERS = 4
GROUP = 8
FOLD = 4
CHUNKS = 2
INIT_VAR = 4.0
MESH = pl.DeviceIdType.MESH


def exp_digamma(x):
    u = x * (x + 5.0)
    steps = (2.0 * x + 5.0) * ((3.0 * u + 20.0) * u + 24.0) / (u * (u + 4.0) * (u + 6.0))
    y = x + 6.0
    inv = 1.0 / y
    inv2 = inv * inv
    series = inv * 0.5 + inv2 * (1.0 / 12.0 - inv2 * (1.0 / 120.0 - inv2 * (1.0 / 252.0 - inv2 * (1.0 / 240.0))))
    return y * jnp.exp(-(series + steps))


FLOOR = 2.0**-10
LIMIT = 300.0
STEPS = 32766.0 / math.log2(1.0 + LIMIT / FLOOR)


def encode(value):
    size = jnp.log2(1.0 + jnp.abs(value) * (1.0 / FLOOR)) * STEPS + 0.5
    code = size.astype(jnp.int32)
    return jnp.where(value < 0.0, -code, code).astype(jnp.int16)


def decode(code):
    code = code.astype(jnp.float32)
    size = jnp.exp2(jnp.abs(code) * (1.0 / STEPS)) * FLOOR - FLOOR
    return jnp.where(code < 0.0, -size, size)


def send(src, dst, send_sem, recv_sem, where):
    return pltpu.make_async_remote_copy(
        src_ref=src, dst_ref=dst, send_sem=send_sem, recv_sem=recv_sem, device_id=where, device_id_type=MESH
    )


def flipped(index, mask):
    bit = 1
    while bit <= mask:
        if mask & bit:
            index = index + bit - 2 * bit * lax.rem(index // bit, 2)
        bit *= 2
    return index


def kernel(
    n_tm,
    n_doc,
    beta_hbm,
    ids_hbm,
    cnt_hbm,
    slot_hbm,
    prior_hbm,
    prec_hbm,
    drift_hbm,
    coded,
    topics_ref,
    beta_ref,
    ids_ref,
    cnt_ref,
    slot_ref,
    prior_ref,
    prec_ref,
    drift_ref,
    load_sem,
    msg,
    land,
    table,
    expo,
    scale,
    quarter,
    weighted,
    counts,
    alpha,
    part,
    sums,
    end_part,
    end_sums,
    gain,
    back,
    share,
    pseudo,
    years_in,
    local,
    mid_out,
    mid_in,
    years_out,
    msg_send,
    msg_recv,
    sum_send,
    sum_recv,
    end_send,
    end_recv,
    in_send,
    in_recv,
    mid_send,
    mid_recv,
    out_send,
    out_recv,
):
    me = lax.axis_index("doc")
    t = lax.axis_index("tm")
    n_blocks = n_tm // GROUP
    b = t // GROUP
    m = lax.rem(t, GROUP)
    own = beta_ref.shape[0]
    dpd = ids_ref.shape[0]
    held = dpd * 128
    span = own // GROUP
    width = span // CHUNKS

    def partners(index, count, order):
        return [(mask, flipped(index, mask)) for mask in order if mask < count]

    peers = partners(me, n_doc, (5, 3, 7, 4, 1, 2, 6))
    mates = partners(m, GROUP, (7, 6, 5, 4, 3, 2, 1))
    others = partners(b, n_blocks, (2, 1, 3))

    def mate_id(mate):
        return {"tm": b * GROUP + mate}

    def other_id(other):
        return {"tm": other * GROUP + m}

    barrier = pltpu.get_barrier_semaphore()
    for _, peer in peers:
        pl.semaphore_signal(barrier, inc=1, device_id={"doc": peer}, device_id_type=MESH)
    for _, other in others:
        pl.semaphore_signal(barrier, inc=1, device_id=other_id(other), device_id_type=MESH)
    for _, mate in mates:
        pl.semaphore_signal(barrier, inc=1, device_id=mate_id(mate), device_id_type=MESH)

    loads = [
        pltpu.make_async_copy(source, held_here, load_sem.at[k])
        for k, (source, held_here) in enumerate(
            [
                (ids_hbm, ids_ref),
                (slot_hbm, slot_ref),
                (cnt_hbm, cnt_ref),
                (beta_hbm, beta_ref),
                (prec_hbm, prec_ref),
                (drift_hbm, drift_ref),
                (prior_hbm, prior_ref),
            ]
        )
    ]
    for load in loads:
        load.start()
    for load in loads:
        load.wait()

    ids = ids_ref[...]
    block_of = lax.shift_right_logical(ids, 7)
    inside = jnp.bitwise_and(ids, 127)
    place = jnp.zeros_like(ids)
    for k in range(slot_ref.shape[0]):
        place = jnp.where(block_of == k, slot_ref[k], place)
    columns = (place * BLOCK + inside).astype(jnp.float32)
    beta = beta_ref[...]
    peak = jnp.max(beta, axis=0, keepdims=True)
    total = jnp.sum(jnp.exp(beta - peak), axis=0, keepdims=True)
    msg[...] = jnp.zeros_like(msg)
    msg[0:dpd, :] = columns
    msg[dpd : dpd + 1, :] = peak
    msg[dpd + 1 : dpd + 2, :] = total
    msg[8 : 8 + dpd, :] = cnt_ref[...].astype(jnp.float32)
    land[me] = msg[...]

    pl.semaphore_wait(barrier, len(peers) + len(mates) + len(others))

    def msg_copy(off, peer, source):
        return send(msg, land.at[source], msg_send.at[off], msg_recv.at[source], {"doc": peer})

    for off, peer in peers:
        msg_copy(off, peer, me).start()

    drift = drift_ref[...]
    var = jnp.full_like(drift, INIT_VAR)
    filt = []
    for k in range(n_tm):
        precision = prec_ref[k : k + 1, :]
        inverse = 1.0 / (1.0 + var * precision)
        gain[k : k + 1, :] = var * precision * inverse
        filt.append(var * inverse)
        var = filt[k] + drift
    info = jnp.zeros_like(drift)
    for k in reversed(range(n_tm)):
        share[k : k + 1, :] = 1.0 / (1.0 + filt[k] * info)
        precision = prec_ref[k : k + 1, :]
        merged = info + precision
        back[k : k + 1, :] = precision / merged
        info = merged / (1.0 + drift * merged)
    prior = prior_ref[...]

    for off, peer in peers:
        msg_copy(off, peer, peer).wait_recv()

    peaks = [land[s, dpd : dpd + 1, :] for s in range(n_doc)]
    peak = functools.reduce(jnp.maximum, peaks)
    total = sum(land[s, dpd + 1 : dpd + 2, :] * jnp.exp(peaks[s] - peak) for s in range(n_doc))
    normalizer = peak + jnp.log(total)
    fold = own // FOLD
    for f in range(FOLD):
        table[:, f * K : (f + 1) * K] = (beta_ref[f * fold : (f + 1) * fold, :] - normalizer).astype(jnp.bfloat16)

    base = (me * own).astype(jnp.float32)
    lanes = lax.broadcasted_iota(jnp.int32, (128, 128), 1).astype(jnp.float32)

    for s in range(n_doc):
        start = jnp.sum(land[s, 8 : 8 + dpd, :], axis=1, keepdims=True) / K
        row = (s % (n_doc // 2)) * dpd
        alpha[s // (n_doc // 2), row : row + dpd, :] = jnp.broadcast_to(start, (dpd, K))
    alpha[...] = exp_digamma(prior + alpha[...])

    def look_up(s, _):
        marks, parts = [], []
        for i in range(dpd):
            both = land[s, pl.ds(i, 1), :] * 16.0 + land[s, pl.ds(8 + i, 1), :]
            both = jnp.transpose(jnp.broadcast_to(both, (128, 128)))
            col = jnp.floor(both * (1.0 / 16.0))
            cnt = both - 16.0 * col
            col = col - base
            part_of = jnp.floor(col * (1.0 / fold))
            rest = col - float(fold) * part_of
            parts.append(part_of)
            at = pl.ds(pl.multiple_of((s * dpd + i) * 128, 128), 128)
            scale[at, :] = jnp.where((part_of >= 0.0) & (part_of < float(FOLD)), cnt, 0.0)
            quarter[at, :] = part_of
            marks.append(
                jnp.concatenate(
                    [(rest == lanes + float(128 * j)).astype(jnp.bfloat16) for j in range(fold // 128)], axis=1
                )
            )
        wide = jnp.dot(jnp.concatenate(marks, axis=0), table[...], preferred_element_type=jnp.float32)
        part_of = jnp.concatenate(parts, axis=0)
        looked = wide[:, 0:K]
        for f in range(1, FOLD):
            looked = jnp.where(part_of == float(f), wide[:, f * K : (f + 1) * K], looked)
        at = pl.ds(pl.multiple_of(s * held, held), held)
        expo[at, :] = jnp.exp(looked - jnp.max(looked, axis=1, keepdims=True))
        return 0

    def sum_copy(sweep, half, off, peer, source):
        turn = 2 * sweep + half
        return send(
            part.at[sweep, half], sums.at[sweep, source, half], sum_send.at[turn, off], sum_recv.at[turn, source], {"doc": peer}
        )

    def end_copy(off, peer, source):
        return send(end_part.at[peer], end_sums.at[source], end_send.at[off], end_recv.at[source], {"doc": peer})

    def word_rows(mate, c):
        return pl.ds(pl.multiple_of(mate * span + c * width, width), width)

    def in_copy(c, mate, source):
        return send(
            pseudo.at[word_rows(mate, c), :], years_in.at[c, source], in_send.at[c, mate], in_recv.at[c, source], mate_id(mate)
        )

    side = n_doc // 2
    spans = fold // span
    words = lax.broadcasted_iota(jnp.int32, (width, 128), 0).astype(jnp.float32)

    def tally(half, c):
        marks = []
        for s in range(half * side, (half + 1) * side):
            rest = land[s, 0:dpd, :] - base
            rest = rest - float(fold) * jnp.floor(rest * (1.0 / fold))
            for i in range(dpd):
                marks.append(
                    jnp.concatenate(
                        [
                            (words + float(h * span + c * width) == rest[i : i + 1, :]).astype(jnp.bfloat16)
                            for h in range(spans)
                        ],
                        axis=0,
                    )
                )
        docs = slice(half * side * held, (half + 1) * side * held)
        found = jnp.dot(jnp.concatenate(marks, axis=1), weighted[docs, :], preferred_element_type=jnp.float32)
        if half == 0:
            counts[c] = found
            return
        for h in range(spans):
            for f in range(FOLD):
                mate = f * spans + h
                first = mate * span + c * width
                rows, columns = slice(h * width, (h + 1) * width), slice(f * K, (f + 1) * K)
                whole = counts[c, rows, columns] + found[rows, columns]
                pseudo[first : first + width, :] = encode(beta_ref[first : first + width, :] + jnp.log(1.0 + whole))
        for _, mate in mates:
            in_copy(c, mate, m).start()

    for sweep in range(EITERS):
        last = sweep == EITERS - 1
        for half in range(2):
            if sweep == 0:
                lax.fori_loop(half * side, (half + 1) * side, look_up, 0, unroll=side)
            else:
                for off, peer in reversed(peers):
                    sum_copy(sweep - 1, half, off, peer, peer).wait_recv()
                whole = sums[sweep - 1, 0, half]
                for s in range(1, n_doc):
                    whole = whole + sums[sweep - 1, s, half]
                alpha[half] = exp_digamma(prior + whole)

            def e_step(s, _, last=last, sweep=sweep, half=half):
                for i in range(dpd):
                    row = s * dpd + i
                    at = pl.ds(pl.multiple_of((half * side * dpd + row) * 128, 128), 128)
                    scaled = expo[at, :] * alpha[half, pl.ds(row, 1), :]
                    scaled = scaled * (scale[at, :] * (1.0 / jnp.sum(scaled, axis=1, keepdims=True)))
                    if last:
                        end_part[half * side + s, i : i + 1, :] = jnp.sum(scaled, axis=0, keepdims=True)
                        for f in range(FOLD):
                            weighted[at, f * K : (f + 1) * K] = jnp.where(quarter[at, :] == float(f), scaled, 0.0).astype(
                                jnp.bfloat16
                            )
                    else:
                        part[sweep, half, pl.ds(row, 1), :] = jnp.sum(scaled, axis=0, keepdims=True)
                return 0

            lax.fori_loop(0, side, e_step, 0, unroll=side)
            if not last:
                for off, peer in peers:
                    sum_copy(sweep, half, off, peer, me).start()
                sums[sweep, me, half] = part[sweep, half]
            else:
                for c in range(CHUNKS):
                    tally(half, c)

    for off, peer in peers:
        end_copy(off, peer, me).start()
    end_sums[me] = end_part[me]

    first_year = b * GROUP
    g = [gain[pl.ds(first_year + i, 1), :] for i in range(GROUP)]
    r = [back[pl.ds(first_year + i, 1), :] for i in range(GROUP)]
    w = [share[pl.ds(first_year + i, 1), :] for i in range(GROUP)]
    keep = []
    for i in range(GROUP):
        keep.append((1.0 - g[i]) * keep[-1] if i else 1.0 - g[i])
    hold = [jnp.ones_like(g[0])]
    for i in reversed(range(GROUP)):
        hold.insert(0, (1.0 - r[i]) * hold[0])
    block_keep, block_hold = [], []
    for other in range(n_blocks):
        years = range(other * GROUP, (other + 1) * GROUP)
        block_keep.append(functools.reduce(jnp.multiply, [1.0 - gain[y : y + 1, :] for y in years]))
        block_hold.append(functools.reduce(jnp.multiply, [1.0 - back[y : y + 1, :] for y in years]))
    into = []
    for other in range(n_blocks):
        fore = jnp.where(other < b, 1.0, 0.0)
        for between in range(other + 1, n_blocks):
            fore = fore * jnp.where(between < b, block_keep[between], 1.0)
        hind = jnp.where(other > b, 1.0, 0.0)
        for between in range(other):
            hind = hind * jnp.where(between > b, block_hold[between], 1.0)
        into.append((fore, hind))

    def mid_copy(c, off, other, source):
        which = jnp.where(other > b, 0, 1)
        return send(mid_out.at[c, which], mid_in.at[c, source], mid_send.at[c, off], mid_recv.at[c, source], other_id(other))

    for off, peer in peers:
        msg_copy(off, peer, me).wait_send()
        for sweep in range(EITERS - 1):
            for half in range(2):
                sum_copy(sweep, half, off, peer, me).wait_send()

    for c in range(CHUNKS):
        years_in[c, m] = pseudo[word_rows(m, c), :]
        mid_in[c, b] = jnp.zeros((width, K), jnp.int16)
        for off, mate in mates:
            in_copy(c, mate, mate).wait_recv()
        values = [decode(years_in[c, i]) for i in range(GROUP)]
        ahead = g[0] * values[0]
        local[c, 0] = w[0] * ahead
        for i in range(1, GROUP):
            ahead = g[i] * values[i] + (1.0 - g[i]) * ahead
            local[c, i] = w[i] * ahead
        mid_out[c, 0] = encode(ahead)
        behind = r[GROUP - 1] * values[GROUP - 1]
        for i in reversed(range(GROUP - 1)):
            local[c, i] += (1.0 - w[i]) * behind
            behind = r[i] * values[i] + (1.0 - r[i]) * behind
        mid_out[c, 1] = encode(behind)
        for off, other in others:
            mid_copy(c, off, other, b).start()

    for off, peer in peers:
        end_copy(off, peer, peer).wait_recv()
    whole = end_sums[0]
    for s in range(1, n_doc):
        whole = whole + end_sums[s]
    topics_ref[...] = prior + whole

    for off, peer in peers:
        end_copy(off, peer, me).wait_send()
    for c in range(CHUNKS):
        for off, mate in mates:
            in_copy(c, mate, m).wait_send()

    def out_copy(c, mate, source):
        return send(
            years_out.at[c, mate], coded.at[word_rows(source, c), :], out_send.at[c, mate], out_recv.at[c, source], mate_id(mate)
        )

    for c in range(CHUNKS):
        for off, other in others:
            mid_copy(c, off, other, other).wait_recv()
        ahead, behind = 0.0, 0.0
        for other in range(n_blocks):
            value = decode(mid_in[c, other])
            ahead = ahead + into[other][0] * value
            behind = behind + into[other][1] * value
        for i in range(GROUP):
            years_out[c, i] = encode(local[c, i] + (w[i] * keep[i]) * ahead + ((1.0 - w[i]) * hold[i + 1]) * behind)
        for off, mate in mates:
            out_copy(c, mate, m).start()
        coded[word_rows(m, c), :] = years_out[c, m]

    for c in range(CHUNKS):
        for off, other in others:
            mid_copy(c, off, other, b).wait_send()
    for c in range(CHUNKS):
        for off, mate in mates:
            out_copy(c, mate, mate).wait_recv()
    for c in range(CHUNKS):
        for off, mate in mates:
            out_copy(c, mate, m).wait_send()


def vmem():
    return pl.BlockSpec(memory_space=pltpu.VMEM)


def solution(mesh):
    n_tm, n_doc = mesh.shape["tm"], mesh.shape["doc"]

    def body(beta, word_ids, word_counts, block_slot, topic_prior, drift_var, obs_precision):
        local_beta, ids, cnt = beta[0], word_ids[0], word_counts[0]
        own, dpd = local_beta.shape[0], ids.shape[0]
        held = dpd * 128
        width = own // GROUP // CHUNKS
        n_blocks = n_tm // GROUP
        f32, bf16, link = jnp.float32, jnp.bfloat16, jnp.int16
        dma = pltpu.SemaphoreType.DMA
        smoothed, doc_topics = pl.pallas_call(
            functools.partial(kernel, n_tm, n_doc),
            out_shape=(jax.ShapeDtypeStruct((own, K), link), jax.ShapeDtypeStruct((dpd, K), f32)),
            in_specs=[pl.BlockSpec(memory_space=pltpu.HBM)] * 7,
            out_specs=(vmem(), vmem()),
            scratch_shapes=[
                pltpu.VMEM((own, K), f32),
                pltpu.VMEM((dpd, 128), jnp.int32),
                pltpu.VMEM((dpd, 128), jnp.int32),
                pltpu.SMEM(block_slot.shape, jnp.int32),
                pltpu.VMEM((1, K), f32),
                pltpu.VMEM((n_tm, K), f32),
                pltpu.VMEM((1, K), f32),
                dma((7,)),
                pltpu.VMEM((16, K), f32),
                pltpu.VMEM((n_doc, 16, K), f32),
                pltpu.VMEM((own // FOLD, FOLD * K), bf16),
                pltpu.VMEM((n_doc * held, K), f32),
                pltpu.VMEM((n_doc * held, K), f32),
                pltpu.VMEM((n_doc * held, K), f32),
                pltpu.VMEM((n_doc * held, FOLD * K), bf16),
                pltpu.VMEM((CHUNKS, own // FOLD // CHUNKS, FOLD * K), f32),
                pltpu.VMEM((2, n_doc // 2 * dpd, K), f32),
                pltpu.VMEM((EITERS - 1, 2, n_doc // 2 * dpd, K), f32),
                pltpu.VMEM((EITERS - 1, n_doc, 2, n_doc // 2 * dpd, K), f32),
                pltpu.VMEM((n_doc, dpd, K), f32),
                pltpu.VMEM((n_doc, dpd, K), f32),
                pltpu.VMEM((n_tm, K), f32),
                pltpu.VMEM((n_tm, K), f32),
                pltpu.VMEM((n_tm, K), f32),
                pltpu.VMEM((own, K), link),
                pltpu.VMEM((CHUNKS, GROUP, width, K), link),
                pltpu.VMEM((CHUNKS, GROUP, width, K), f32),
                pltpu.VMEM((CHUNKS, 2, width, K), link),
                pltpu.VMEM((CHUNKS, n_blocks, width, K), link),
                pltpu.VMEM((CHUNKS, GROUP, width, K), link),
                dma((n_doc,)),
                dma((n_doc,)),
                dma((2 * EITERS - 2, n_doc)),
                dma((2 * EITERS - 2, n_doc)),
                dma((n_doc,)),
                dma((n_doc,)),
                dma((CHUNKS, GROUP)),
                dma((CHUNKS, GROUP)),
                dma((CHUNKS, n_blocks)),
                dma((CHUNKS, n_blocks)),
                dma((CHUNKS, GROUP)),
                dma((CHUNKS, GROUP)),
            ],
            compiler_params=pltpu.CompilerParams(
                collective_id=0, has_side_effects=True, vmem_limit_bytes=48 * 1024 * 1024
            ),
            name="topics",
        )(*[
            pltpu.with_memory_space_constraint(a, pltpu.HBM)
            for a in (local_beta, ids, cnt, block_slot, topic_prior[None], obs_precision, drift_var[None])
        ])
        return (decode(smoothed)[None], doc_topics[None])

    in_specs = (P("tm", "doc", None), P("tm", "doc", None), P("tm", "doc", None), P(), P(), P(), P())
    out_specs = (P("tm", "doc", None), P("tm", "doc", None))
    return jax.shard_map(body, mesh=mesh, in_specs=in_specs, out_specs=out_specs, check_vma=False)
```

```python
import functools
import math

import jax
import jax.numpy as jnp
from jax import lax
from jax.experimental import pallas as pl
from jax.experimental.pallas import tpu as pltpu
from jax.sharding import PartitionSpec as P

K = 128
BLOCK = 128
EITERS = 4
GROUP = 8
FOLD = 4
PARTS = 2
CHUNKS = 4
INIT_VAR = 4.0
MESH = pl.DeviceIdType.MESH


def exp_digamma(x):
    u = x * (x + 5.0)
    steps = (2.0 * x + 5.0) * ((3.0 * u + 20.0) * u + 24.0) / (u * (u + 4.0) * (u + 6.0))
    y = x + 6.0
    inv = 1.0 / y
    inv2 = inv * inv
    series = inv * 0.5 + inv2 * (1.0 / 12.0 - inv2 * (1.0 / 120.0 - inv2 * (1.0 / 252.0 - inv2 * (1.0 / 240.0))))
    return y * jnp.exp(-(series + steps))


FLOOR = 2.0**-10
LIMIT = 300.0
STEPS = 32766.0 / math.log2(1.0 + LIMIT / FLOOR)


def encode(value):
    size = jnp.log2(1.0 + jnp.abs(value) * (1.0 / FLOOR)) * STEPS + 0.5
    code = size.astype(jnp.int32)
    return jnp.where(value < 0.0, -code, code).astype(jnp.int16)


def decode(code):
    code = code.astype(jnp.float32)
    size = jnp.exp2(jnp.abs(code) * (1.0 / STEPS)) * FLOOR - FLOOR
    return jnp.where(code < 0.0, -size, size)


def send(src, dst, send_sem, recv_sem, where):
    return pltpu.make_async_remote_copy(
        src_ref=src, dst_ref=dst, send_sem=send_sem, recv_sem=recv_sem, device_id=where, device_id_type=MESH
    )


def flipped(index, mask):
    bit = 1
    while bit <= mask:
        if mask & bit:
            index = index + bit - 2 * bit * lax.rem(index // bit, 2)
        bit *= 2
    return index


def kernel(
    n_tm,
    n_doc,
    beta_hbm,
    ids_hbm,
    cnt_hbm,
    slot_hbm,
    prior_hbm,
    prec_hbm,
    drift_hbm,
    out_ref,
    topics_ref,
    beta_ref,
    ids_ref,
    cnt_ref,
    slot_ref,
    prior_ref,
    prec_ref,
    drift_ref,
    load_sem,
    msg,
    land,
    table,
    expo,
    scale,
    quarter,
    weighted,
    counts,
    alpha,
    part,
    sums,
    end_part,
    end_sums,
    gain,
    back,
    share,
    pseudo,
    years_in,
    local,
    mid_out,
    mid_in,
    years_out,
    coded,
    msg_send,
    msg_recv,
    sum_send,
    sum_recv,
    end_send,
    end_recv,
    in_send,
    in_recv,
    mid_send,
    mid_recv,
    out_send,
    out_recv,
):
    me = lax.axis_index("doc")
    t = lax.axis_index("tm")
    parts = min(PARTS, n_doc)
    side = n_doc // parts
    n_blocks = n_tm // GROUP
    b = t // GROUP
    m = lax.rem(t, GROUP)
    own = beta_ref.shape[0]
    dpd = ids_ref.shape[0]
    held = dpd * 128
    span = own // GROUP
    width = span // CHUNKS

    def partners(index, count, order):
        return [(mask, flipped(index, mask)) for mask in order if mask < count]

    peers = partners(me, n_doc, (5, 3, 7, 4, 1, 2, 6))
    mates = partners(m, GROUP, (7, 6, 5, 4, 3, 2, 1))
    others = partners(b, n_blocks, (2, 1, 3))

    def mate_id(mate):
        return {"tm": b * GROUP + mate}

    far_bit = GROUP // 2

    def span_of(member):
        return member + (b // 2) * (far_bit - 2 * far_bit * (member // far_bit))

    def other_id(mask, other):
        return {"tm": other * GROUP + (flipped(m, far_bit) if mask & 2 else m)}

    barrier = pltpu.get_barrier_semaphore()
    for _, peer in peers:
        pl.semaphore_signal(barrier, inc=1, device_id={"doc": peer}, device_id_type=MESH)
    for mask, other in others:
        pl.semaphore_signal(barrier, inc=1, device_id=other_id(mask, other), device_id_type=MESH)
    for _, mate in mates:
        pl.semaphore_signal(barrier, inc=1, device_id=mate_id(mate), device_id_type=MESH)

    loads = [
        pltpu.make_async_copy(source, held_here, load_sem.at[k])
        for k, (source, held_here) in enumerate(
            [
                (ids_hbm, ids_ref),
                (slot_hbm, slot_ref),
                (cnt_hbm, cnt_ref),
                (beta_hbm, beta_ref),
                (prec_hbm, prec_ref),
                (drift_hbm, drift_ref),
                (prior_hbm, prior_ref),
            ]
        )
    ]
    for load in loads:
        load.start()
    for load in loads:
        load.wait()

    ids = ids_ref[...]
    block_of = lax.shift_right_logical(ids, 7)
    inside = jnp.bitwise_and(ids, 127)
    place = jnp.zeros_like(ids)
    for k in range(slot_ref.shape[0]):
        place = jnp.where(block_of == k, slot_ref[k], place)
    columns = (place * BLOCK + inside).astype(jnp.float32)
    beta = beta_ref[...]
    peak = jnp.max(beta, axis=0, keepdims=True)
    total = jnp.sum(jnp.exp(beta - peak), axis=0, keepdims=True)
    msg[...] = jnp.zeros_like(msg)
    msg[0:dpd, :] = columns
    msg[dpd : dpd + 1, :] = peak
    msg[dpd + 1 : dpd + 2, :] = total
    msg[8 : 8 + dpd, :] = cnt_ref[...].astype(jnp.float32)
    land[me] = msg[...]

    pl.semaphore_wait(barrier, len(peers) + len(mates) + len(others))

    def msg_copy(off, peer, source):
        return send(msg, land.at[source], msg_send.at[off], msg_recv.at[source], {"doc": peer})

    for off, peer in peers:
        msg_copy(off, peer, me).start()

    drift = drift_ref[...]
    var = jnp.full_like(drift, INIT_VAR)
    filt = []
    for k in range(n_tm):
        precision = prec_ref[k : k + 1, :]
        inverse = 1.0 / (1.0 + var * precision)
        gain[k : k + 1, :] = var * precision * inverse
        filt.append(var * inverse)
        var = filt[k] + drift
    info = jnp.zeros_like(drift)
    for k in reversed(range(n_tm)):
        share[k : k + 1, :] = 1.0 / (1.0 + filt[k] * info)
        precision = prec_ref[k : k + 1, :]
        merged = info + precision
        back[k : k + 1, :] = precision / merged
        info = merged / (1.0 + drift * merged)
    prior = prior_ref[...]

    for off, peer in peers:
        msg_copy(off, peer, peer).wait_recv()

    peaks = [land[s, dpd : dpd + 1, :] for s in range(n_doc)]
    peak = functools.reduce(jnp.maximum, peaks)
    total = sum(land[s, dpd + 1 : dpd + 2, :] * jnp.exp(peaks[s] - peak) for s in range(n_doc))
    normalizer = peak + jnp.log(total)
    fold = own // FOLD
    for f in range(FOLD):
        table[:, f * K : (f + 1) * K] = (beta_ref[f * fold : (f + 1) * fold, :] - normalizer).astype(jnp.bfloat16)

    base = (me * own).astype(jnp.float32)
    lanes = lax.broadcasted_iota(jnp.int32, (128, 128), 1).astype(jnp.float32)

    for s in range(n_doc):
        start = jnp.sum(land[s, 8 : 8 + dpd, :], axis=1, keepdims=True) / K
        row = (s % side) * dpd
        alpha[s // side, row : row + dpd, :] = jnp.broadcast_to(start, (dpd, K))
    alpha[...] = exp_digamma(prior + alpha[...])

    def look_up(s, _):
        marks, parts = [], []
        for i in range(dpd):
            both = land[s, pl.ds(i, 1), :] * 16.0 + land[s, pl.ds(8 + i, 1), :]
            both = jnp.transpose(jnp.broadcast_to(both, (128, 128)))
            col = jnp.floor(both * (1.0 / 16.0))
            cnt = both - 16.0 * col
            col = col - base
            part_of = jnp.floor(col * (1.0 / fold))
            rest = col - float(fold) * part_of
            parts.append(part_of)
            at = pl.ds(pl.multiple_of((s * dpd + i) * 128, 128), 128)
            scale[at, :] = jnp.where((part_of >= 0.0) & (part_of < float(FOLD)), cnt, 0.0)
            quarter[at, :] = part_of
            marks.append(
                jnp.concatenate(
                    [(rest == lanes + float(128 * j)).astype(jnp.bfloat16) for j in range(fold // 128)], axis=1
                )
            )
        wide = jnp.dot(jnp.concatenate(marks, axis=0), table[...], preferred_element_type=jnp.float32)
        part_of = jnp.concatenate(parts, axis=0)
        looked = wide[:, 0:K]
        for f in range(1, FOLD):
            looked = jnp.where(part_of == float(f), wide[:, f * K : (f + 1) * K], looked)
        at = pl.ds(pl.multiple_of(s * held, held), held)
        expo[at, :] = jnp.exp(looked - jnp.max(looked, axis=1, keepdims=True))
        return 0

    def sum_copy(sweep, part_no, off, peer, source):
        turn = parts * sweep + part_no
        return send(
            part.at[sweep, part_no], sums.at[sweep, source, part_no], sum_send.at[turn, off], sum_recv.at[turn, source], {"doc": peer}
        )

    def end_copy(off, peer, source):
        return send(end_part.at[peer], end_sums.at[source], end_send.at[off], end_recv.at[source], {"doc": peer})

    def word_rows(mate, c):
        return pl.ds(pl.multiple_of(span_of(mate) * span + c * width, width), width)

    def in_copy(c, mate, source):
        return send(
            pseudo.at[word_rows(mate, c), :], years_in.at[c, source], in_send.at[c, mate], in_recv.at[c, source], mate_id(mate)
        )

    spans = fold // span
    words = lax.broadcasted_iota(jnp.int32, (width, 128), 0).astype(jnp.float32)

    def tally(part_no, c):
        marks = []
        for s in range(part_no * side, (part_no + 1) * side):
            rest = land[s, 0:dpd, :] - base
            rest = rest - float(fold) * jnp.floor(rest * (1.0 / fold))
            for i in range(dpd):
                marks.append(
                    jnp.concatenate(
                        [
                            (words + float(h * span + c * width) == rest[i : i + 1, :]).astype(jnp.bfloat16)
                            for h in range(spans)
                        ],
                        axis=0,
                    )
                )
        docs = slice(part_no * side * held, (part_no + 1) * side * held)
        found = jnp.dot(jnp.concatenate(marks, axis=1), weighted[docs, :], preferred_element_type=jnp.float32)
        if part_no == 0:
            counts[c] = found
        elif part_no < parts - 1:
            counts[c] += found
        if part_no < parts - 1:
            return
        for h in range(spans):
            for f in range(FOLD):
                mate = f * spans + h
                first = mate * span + c * width
                rows, columns = slice(h * width, (h + 1) * width), slice(f * K, (f + 1) * K)
                whole = counts[c, rows, columns] + found[rows, columns]
                pseudo[first : first + width, :] = encode(beta_ref[first : first + width, :] + jnp.log(1.0 + whole))
        for _, mate in mates:
            in_copy(c, mate, m).start()

    for sweep in range(EITERS):
        last = sweep == EITERS - 1
        for part_no in range(parts):
            if sweep == 0:
                lax.fori_loop(part_no * side, (part_no + 1) * side, look_up, 0, unroll=side)
            else:
                for off, peer in reversed(peers):
                    sum_copy(sweep - 1, part_no, off, peer, peer).wait_recv()
                whole = sums[sweep - 1, 0, part_no]
                for s in range(1, n_doc):
                    whole = whole + sums[sweep - 1, s, part_no]
                alpha[part_no] = exp_digamma(prior + whole)

            def e_step(s, _, last=last, sweep=sweep, part_no=part_no):
                for i in range(dpd):
                    row = s * dpd + i
                    at = pl.ds(pl.multiple_of((part_no * side * dpd + row) * 128, 128), 128)
                    scaled = expo[at, :] * alpha[part_no, pl.ds(row, 1), :]
                    scaled = scaled * (scale[at, :] * (1.0 / jnp.sum(scaled, axis=1, keepdims=True)))
                    if last:
                        end_part[part_no * side + s, i : i + 1, :] = jnp.sum(scaled, axis=0, keepdims=True)
                        for f in range(FOLD):
                            weighted[at, f * K : (f + 1) * K] = jnp.where(quarter[at, :] == float(f), scaled, 0.0).astype(
                                jnp.bfloat16
                            )
                    else:
                        part[sweep, part_no, pl.ds(row, 1), :] = jnp.sum(scaled, axis=0, keepdims=True)
                return 0

            lax.fori_loop(0, side, e_step, 0, unroll=side)
            if not last:
                for off, peer in peers:
                    sum_copy(sweep, part_no, off, peer, me).start()
                sums[sweep, me, part_no] = part[sweep, part_no]
            else:
                for c in range(CHUNKS):
                    tally(part_no, c)

    for off, peer in peers:
        end_copy(off, peer, me).start()
    end_sums[me] = end_part[me]

    first_year = b * GROUP
    g = [gain[pl.ds(first_year + i, 1), :] for i in range(GROUP)]
    r = [back[pl.ds(first_year + i, 1), :] for i in range(GROUP)]
    w = [share[pl.ds(first_year + i, 1), :] for i in range(GROUP)]
    keep = []
    for i in range(GROUP):
        keep.append((1.0 - g[i]) * keep[-1] if i else 1.0 - g[i])
    hold = [jnp.ones_like(g[0])]
    for i in reversed(range(GROUP)):
        hold.insert(0, (1.0 - r[i]) * hold[0])
    block_keep, block_hold = [], []
    for other in range(n_blocks):
        years = range(other * GROUP, (other + 1) * GROUP)
        block_keep.append(functools.reduce(jnp.multiply, [1.0 - gain[y : y + 1, :] for y in years]))
        block_hold.append(functools.reduce(jnp.multiply, [1.0 - back[y : y + 1, :] for y in years]))
    into = []
    for other in range(n_blocks):
        fore = jnp.where(other < b, 1.0, 0.0)
        for between in range(other + 1, n_blocks):
            fore = fore * jnp.where(between < b, block_keep[between], 1.0)
        hind = jnp.where(other > b, 1.0, 0.0)
        for between in range(other):
            hind = hind * jnp.where(between > b, block_hold[between], 1.0)
        into.append((fore, hind))

    def mid_copy(c, off, other, source):
        which = jnp.where(other > b, 0, 1)
        return send(mid_out.at[c, which], mid_in.at[c, source], mid_send.at[c, off], mid_recv.at[c, source], other_id(off, other))

    for off, peer in peers:
        msg_copy(off, peer, me).wait_send()
        for sweep in range(EITERS - 1):
            for part_no in range(parts):
                sum_copy(sweep, part_no, off, peer, me).wait_send()

    for c in range(CHUNKS):
        years_in[c, m] = pseudo[word_rows(m, c), :]
        mid_in[c, b] = jnp.zeros((width, K), jnp.int16)
        for off, mate in mates:
            in_copy(c, mate, mate).wait_recv()
        values = [decode(years_in[c, i]) for i in range(GROUP)]
        ahead = g[0] * values[0]
        local[c, 0] = w[0] * ahead
        for i in range(1, GROUP):
            ahead = g[i] * values[i] + (1.0 - g[i]) * ahead
            local[c, i] = w[i] * ahead
        mid_out[c, 0] = encode(ahead)
        behind = r[GROUP - 1] * values[GROUP - 1]
        for i in reversed(range(GROUP - 1)):
            local[c, i] += (1.0 - w[i]) * behind
            behind = r[i] * values[i] + (1.0 - r[i]) * behind
        mid_out[c, 1] = encode(behind)
        for off, other in others:
            mid_copy(c, off, other, b).start()

    for off, peer in peers:
        end_copy(off, peer, peer).wait_recv()
    whole = end_sums[0]
    for s in range(1, n_doc):
        whole = whole + end_sums[s]
    topics_ref[...] = prior + whole

    for off, peer in peers:
        end_copy(off, peer, me).wait_send()
    for c in range(CHUNKS):
        for off, mate in mates:
            in_copy(c, mate, m).wait_send()

    def out_copy(c, mate, source):
        return send(
            years_out.at[c, mate], coded.at[word_rows(source, c), :], out_send.at[c, mate], out_recv.at[c, source], mate_id(mate)
        )

    for c in range(CHUNKS):
        for off, other in others:
            mid_copy(c, off, other, other).wait_recv()
        ahead, behind = 0.0, 0.0
        for other in range(n_blocks):
            value = decode(mid_in[c, other])
            ahead = ahead + into[other][0] * value
            behind = behind + into[other][1] * value
        for i in range(GROUP):
            years_out[c, i] = encode(local[c, i] + (w[i] * keep[i]) * ahead + ((1.0 - w[i]) * hold[i + 1]) * behind)
        for off, mate in mates:
            out_copy(c, mate, m).start()
        out_ref[word_rows(m, c), :] = decode(years_out[c, m])

    for c in range(CHUNKS):
        for off, other in others:
            mid_copy(c, off, other, b).wait_send()
    for c in range(CHUNKS):
        for off, mate in mates:
            out_copy(c, mate, mate).wait_recv()
            out_ref[word_rows(mate, c), :] = decode(coded[word_rows(mate, c), :])
    for c in range(CHUNKS):
        for off, mate in mates:
            out_copy(c, mate, m).wait_send()


def vmem():
    return pl.BlockSpec(memory_space=pltpu.VMEM)


def solution(mesh):
    n_tm, n_doc = mesh.shape["tm"], mesh.shape["doc"]

    def body(beta, word_ids, word_counts, block_slot, topic_prior, drift_var, obs_precision):
        local_beta, ids, cnt = beta[0], word_ids[0], word_counts[0]
        own, dpd = local_beta.shape[0], ids.shape[0]
        held = dpd * 128
        width = own // GROUP // CHUNKS
        n_blocks = n_tm // GROUP
        parts = min(PARTS, n_doc)
        lot = n_doc // parts * dpd
        f32, bf16, link = jnp.float32, jnp.bfloat16, jnp.int16
        dma = pltpu.SemaphoreType.DMA
        smoothed, doc_topics = pl.pallas_call(
            functools.partial(kernel, n_tm, n_doc),
            out_shape=(jax.ShapeDtypeStruct((own, K), f32), jax.ShapeDtypeStruct((dpd, K), f32)),
            in_specs=[pl.BlockSpec(memory_space=pltpu.HBM)] * 7,
            out_specs=(vmem(), vmem()),
            scratch_shapes=[
                pltpu.VMEM((own, K), f32),
                pltpu.VMEM((dpd, 128), jnp.int32),
                pltpu.VMEM((dpd, 128), jnp.int32),
                pltpu.SMEM(block_slot.shape, jnp.int32),
                pltpu.VMEM((1, K), f32),
                pltpu.VMEM((n_tm, K), f32),
                pltpu.VMEM((1, K), f32),
                dma((7,)),
                pltpu.VMEM((16, K), f32),
                pltpu.VMEM((n_doc, 16, K), f32),
                pltpu.VMEM((own // FOLD, FOLD * K), bf16),
                pltpu.VMEM((n_doc * held, K), f32),
                pltpu.VMEM((n_doc * held, K), f32),
                pltpu.VMEM((n_doc * held, K), f32),
                pltpu.VMEM((n_doc * held, FOLD * K), bf16),
                pltpu.VMEM((CHUNKS, own // FOLD // CHUNKS, FOLD * K), f32),
                pltpu.VMEM((parts, lot, K), f32),
                pltpu.VMEM((EITERS - 1, parts, lot, K), f32),
                pltpu.VMEM((EITERS - 1, n_doc, parts, lot, K), f32),
                pltpu.VMEM((n_doc, dpd, K), f32),
                pltpu.VMEM((n_doc, dpd, K), f32),
                pltpu.VMEM((n_tm, K), f32),
                pltpu.VMEM((n_tm, K), f32),
                pltpu.VMEM((n_tm, K), f32),
                pltpu.VMEM((own, K), link),
                pltpu.VMEM((CHUNKS, GROUP, width, K), link),
                pltpu.VMEM((CHUNKS, GROUP, width, K), f32),
                pltpu.VMEM((CHUNKS, 2, width, K), link),
                pltpu.VMEM((CHUNKS, n_blocks, width, K), link),
                pltpu.VMEM((CHUNKS, GROUP, width, K), link),
                pltpu.VMEM((own, K), link),
                dma((n_doc,)),
                dma((n_doc,)),
                dma((parts * (EITERS - 1), n_doc)),
                dma((parts * (EITERS - 1), n_doc)),
                dma((n_doc,)),
                dma((n_doc,)),
                dma((CHUNKS, GROUP)),
                dma((CHUNKS, GROUP)),
                dma((CHUNKS, n_blocks)),
                dma((CHUNKS, n_blocks)),
                dma((CHUNKS, GROUP)),
                dma((CHUNKS, GROUP)),
            ],
            compiler_params=pltpu.CompilerParams(
                collective_id=0, has_side_effects=True, vmem_limit_bytes=48 * 1024 * 1024
            ),
            name="topics",
        )(*[
            pltpu.with_memory_space_constraint(a, pltpu.HBM)
            for a in (local_beta, ids, cnt, block_slot, topic_prior[None], obs_precision, drift_var[None])
        ])
        return (smoothed[None], doc_topics[None])

    in_specs = (P("tm", "doc", None), P("tm", "doc", None), P("tm", "doc", None), P(), P(), P(), P())
    out_specs = (P("tm", "doc", None), P("tm", "doc", None))
    return jax.shard_map(body, mesh=mesh, in_specs=in_specs, out_specs=out_specs, check_vma=False)
```

```python
import functools
import math

import jax
import jax.numpy as jnp
from jax import lax
from jax.experimental import pallas as pl
from jax.experimental.pallas import tpu as pltpu
from jax.sharding import PartitionSpec as P

K = 128
BLOCK = 128
EITERS = 4
GROUP = 8
FOLD = 4
PARTS = 2
CHUNKS = 4
INIT_VAR = 4.0
MESH = pl.DeviceIdType.MESH


def exp_digamma(x):
    u = x * (x + 5.0)
    steps = (2.0 * x + 5.0) * ((3.0 * u + 20.0) * u + 24.0) / (u * (u + 4.0) * (u + 6.0))
    y = x + 6.0
    inv = 1.0 / y
    inv2 = inv * inv
    series = inv * 0.5 + inv2 * (1.0 / 12.0 - inv2 * (1.0 / 120.0 - inv2 * (1.0 / 252.0 - inv2 * (1.0 / 240.0))))
    return y * jnp.exp(-(series + steps))


FLOOR = 2.0**-10
LIMIT = 300.0
STEPS = 32766.0 / math.log2(1.0 + LIMIT / FLOOR)


def encode(value):
    size = jnp.log2(1.0 + jnp.abs(value) * (1.0 / FLOOR)) * STEPS + 0.5
    code = size.astype(jnp.int32)
    return jnp.where(value < 0.0, -code, code).astype(jnp.int16)


def decode(code):
    code = code.astype(jnp.float32)
    size = jnp.exp2(jnp.abs(code) * (1.0 / STEPS)) * FLOOR - FLOOR
    return jnp.where(code < 0.0, -size, size)


def send(src, dst, send_sem, recv_sem, where):
    return pltpu.make_async_remote_copy(
        src_ref=src, dst_ref=dst, send_sem=send_sem, recv_sem=recv_sem, device_id=where, device_id_type=MESH
    )


def flipped(index, mask):
    bit = 1
    while bit <= mask:
        if mask & bit:
            index = index + bit - 2 * bit * lax.rem(index // bit, 2)
        bit *= 2
    return index


def kernel(
    n_tm,
    n_doc,
    beta_hbm,
    ids_hbm,
    cnt_hbm,
    slot_hbm,
    prior_hbm,
    prec_hbm,
    drift_hbm,
    out_ref,
    topics_ref,
    beta_ref,
    ids_ref,
    cnt_ref,
    slot_ref,
    prior_ref,
    prec_ref,
    drift_ref,
    load_sem,
    msg,
    land,
    table,
    expo,
    scale,
    quarter,
    weighted,
    counts,
    alpha,
    part,
    sums,
    end_part,
    end_sums,
    gain,
    back,
    share,
    pseudo,
    years_in,
    local,
    mid_out,
    mid_in,
    years_out,
    coded,
    msg_send,
    msg_recv,
    sum_send,
    sum_recv,
    end_send,
    end_recv,
    in_send,
    in_recv,
    mid_send,
    mid_recv,
    out_send,
    out_recv,
):
    me = lax.axis_index("doc")
    t = lax.axis_index("tm")
    parts = min(PARTS, n_doc)
    side = n_doc // parts
    n_blocks = n_tm // GROUP
    b = t // GROUP
    m = lax.rem(t, GROUP)
    own = beta_ref.shape[0]
    dpd = ids_ref.shape[0]
    held = dpd * 128
    span = own // GROUP
    width = span // CHUNKS

    def partners(index, count, order):
        return [(mask, flipped(index, mask)) for mask in order if mask < count]

    peers = partners(me, n_doc, (5, 3, 7, 4, 1, 2, 6))
    mates = partners(m, GROUP, (7, 6, 5, 4, 3, 2, 1))
    others = partners(b, n_blocks, (2, 1, 3))

    def mate_id(mate):
        return {"tm": b * GROUP + mate}

    far_bit = GROUP // 2

    def span_of(member):
        return member + (b // 2) * (far_bit - 2 * far_bit * (member // far_bit))

    def other_id(mask, other):
        return {"tm": other * GROUP + (flipped(m, far_bit) if mask & 2 else m)}

    barrier = pltpu.get_barrier_semaphore()
    for _, peer in peers:
        pl.semaphore_signal(barrier, inc=1, device_id={"doc": peer}, device_id_type=MESH)
    for mask, other in others:
        pl.semaphore_signal(barrier, inc=1, device_id=other_id(mask, other), device_id_type=MESH)
    for _, mate in mates:
        pl.semaphore_signal(barrier, inc=1, device_id=mate_id(mate), device_id_type=MESH)

    loads = [
        pltpu.make_async_copy(source, held_here, load_sem.at[k])
        for k, (source, held_here) in enumerate(
            [
                (ids_hbm, ids_ref),
                (slot_hbm, slot_ref),
                (cnt_hbm, cnt_ref),
                (beta_hbm, beta_ref),
                (prec_hbm, prec_ref),
                (drift_hbm, drift_ref),
                (prior_hbm, prior_ref),
            ]
        )
    ]
    for load in loads:
        load.start()
    for load in loads:
        load.wait()

    ids = ids_ref[...]
    block_of = lax.shift_right_logical(ids, 7)
    inside = jnp.bitwise_and(ids, 127)
    place = jnp.zeros_like(ids)
    for k in range(slot_ref.shape[0]):
        place = jnp.where(block_of == k, slot_ref[k], place)
    columns = (place * BLOCK + inside).astype(jnp.float32)
    beta = beta_ref[...]
    peak = jnp.max(beta, axis=0, keepdims=True)
    total = jnp.sum(jnp.exp(beta - peak), axis=0, keepdims=True)
    msg[...] = jnp.zeros_like(msg)
    msg[0:dpd, :] = columns
    msg[dpd : dpd + 1, :] = peak
    msg[dpd + 1 : dpd + 2, :] = total
    msg[8 : 8 + dpd, :] = cnt_ref[...].astype(jnp.float32)
    land[me] = msg[...]

    pl.semaphore_wait(barrier, len(peers) + len(mates) + len(others))

    def msg_copy(off, peer, source):
        return send(msg, land.at[source], msg_send.at[off], msg_recv.at[source], {"doc": peer})

    for off, peer in peers:
        msg_copy(off, peer, me).start()

    drift = drift_ref[...]
    var = jnp.full_like(drift, INIT_VAR)
    filt = []
    for k in range(n_tm):
        precision = prec_ref[k : k + 1, :]
        inverse = 1.0 / (1.0 + var * precision)
        gain[k : k + 1, :] = var * precision * inverse
        filt.append(var * inverse)
        var = filt[k] + drift
    info = jnp.zeros_like(drift)
    for k in reversed(range(n_tm)):
        share[k : k + 1, :] = 1.0 / (1.0 + filt[k] * info)
        precision = prec_ref[k : k + 1, :]
        merged = info + precision
        back[k : k + 1, :] = precision / merged
        info = merged / (1.0 + drift * merged)
    prior = prior_ref[...]

    for off, peer in peers:
        msg_copy(off, peer, peer).wait_recv()

    peaks = [land[s, dpd : dpd + 1, :] for s in range(n_doc)]
    peak = functools.reduce(jnp.maximum, peaks)
    total = sum(land[s, dpd + 1 : dpd + 2, :] * jnp.exp(peaks[s] - peak) for s in range(n_doc))
    normalizer = peak + jnp.log(total)
    fold = own // FOLD
    for f in range(FOLD):
        table[:, f * K : (f + 1) * K] = (beta_ref[f * fold : (f + 1) * fold, :] - normalizer).astype(jnp.bfloat16)

    base = (me * own).astype(jnp.float32)
    lanes = lax.broadcasted_iota(jnp.int32, (128, 128), 1).astype(jnp.float32)

    for s in range(n_doc):
        start = jnp.sum(land[s, 8 : 8 + dpd, :], axis=1, keepdims=True) / K
        row = (s % side) * dpd
        alpha[s // side, row : row + dpd, :] = jnp.broadcast_to(start, (dpd, K))
    alpha[...] = exp_digamma(prior + alpha[...])

    def look_up(s, _):
        marks, parts = [], []
        for i in range(dpd):
            both = land[s, pl.ds(i, 1), :] * 16.0 + land[s, pl.ds(8 + i, 1), :]
            both = jnp.transpose(jnp.broadcast_to(both, (128, 128)))
            col = jnp.floor(both * (1.0 / 16.0))
            cnt = both - 16.0 * col
            col = col - base
            part_of = jnp.floor(col * (1.0 / fold))
            rest = col - float(fold) * part_of
            parts.append(part_of)
            at = pl.ds(pl.multiple_of((s * dpd + i) * 128, 128), 128)
            scale[at, :] = jnp.where((part_of >= 0.0) & (part_of < float(FOLD)), cnt, 0.0)
            quarter[at, :] = part_of
            marks.append(
                jnp.concatenate(
                    [(rest == lanes + float(128 * j)).astype(jnp.bfloat16) for j in range(fold // 128)], axis=1
                )
            )
        wide = jnp.dot(jnp.concatenate(marks, axis=0), table[...], preferred_element_type=jnp.float32)
        part_of = jnp.concatenate(parts, axis=0)
        looked = wide[:, 0:K]
        for f in range(1, FOLD):
            looked = jnp.where(part_of == float(f), wide[:, f * K : (f + 1) * K], looked)
        at = pl.ds(pl.multiple_of(s * held, held), held)
        expo[at, :] = jnp.exp(looked - jnp.max(looked, axis=1, keepdims=True))
        return 0

    def sum_copy(sweep, part_no, off, peer, source):
        turn = parts * sweep + part_no
        return send(
            part.at[sweep, part_no], sums.at[sweep, source, part_no], sum_send.at[turn, off], sum_recv.at[turn, source], {"doc": peer}
        )

    def end_copy(off, peer, source):
        return send(end_part.at[peer], end_sums.at[source], end_send.at[off], end_recv.at[source], {"doc": peer})

    def word_rows(mate, c):
        return pl.ds(pl.multiple_of(span_of(mate) * span + c * width, width), width)

    def in_copy(c, mate, source):
        return send(
            pseudo.at[word_rows(mate, c), :], years_in.at[c, source], in_send.at[c, mate], in_recv.at[c, source], mate_id(mate)
        )

    spans = fold // span
    words = lax.broadcasted_iota(jnp.int32, (width, 128), 0).astype(jnp.float32)

    def tally(part_no, c):
        marks = []
        for s in range(part_no * side, (part_no + 1) * side):
            rest = land[s, 0:dpd, :] - base
            rest = rest - float(fold) * jnp.floor(rest * (1.0 / fold))
            for i in range(dpd):
                marks.append(
                    jnp.concatenate(
                        [
                            (words + float(h * span + c * width) == rest[i : i + 1, :]).astype(jnp.bfloat16)
                            for h in range(spans)
                        ],
                        axis=0,
                    )
                )
        docs = slice(part_no * side * held, (part_no + 1) * side * held)
        found = jnp.dot(jnp.concatenate(marks, axis=1), weighted[docs, :], preferred_element_type=jnp.float32)
        if part_no == 0:
            counts[c] = found
        elif part_no < parts - 1:
            counts[c] += found
        if part_no < parts - 1:
            return
        for h in range(spans):
            for f in range(FOLD):
                mate = f * spans + h
                first = mate * span + c * width
                rows, columns = slice(h * width, (h + 1) * width), slice(f * K, (f + 1) * K)
                whole = counts[c, rows, columns] + found[rows, columns]
                pseudo[first : first + width, :] = encode(beta_ref[first : first + width, :] + jnp.log(1.0 + whole))
        for _, mate in mates:
            in_copy(c, mate, m).start()

    for sweep in range(EITERS):
        last = sweep == EITERS - 1
        for part_no in range(parts):
            if sweep == 0:
                lax.fori_loop(part_no * side, (part_no + 1) * side, look_up, 0, unroll=side)
            else:
                for off, peer in reversed(peers):
                    sum_copy(sweep - 1, part_no, off, peer, peer).wait_recv()
                whole = sums[sweep - 1, 0, part_no]
                for s in range(1, n_doc):
                    whole = whole + sums[sweep - 1, s, part_no]
                alpha[part_no] = exp_digamma(prior + whole)

            def e_step(s, _, last=last, sweep=sweep, part_no=part_no):
                for i in range(dpd):
                    row = s * dpd + i
                    at = pl.ds(pl.multiple_of((part_no * side * dpd + row) * 128, 128), 128)
                    scaled = expo[at, :] * alpha[part_no, pl.ds(row, 1), :]
                    scaled = scaled * (scale[at, :] * (1.0 / jnp.sum(scaled, axis=1, keepdims=True)))
                    if last:
                        end_part[part_no * side + s, i : i + 1, :] = jnp.sum(scaled, axis=0, keepdims=True)
                        for f in range(FOLD):
                            weighted[at, f * K : (f + 1) * K] = jnp.where(quarter[at, :] == float(f), scaled, 0.0).astype(
                                jnp.bfloat16
                            )
                    else:
                        part[sweep, part_no, pl.ds(row, 1), :] = jnp.sum(scaled, axis=0, keepdims=True)
                return 0

            lax.fori_loop(0, side, e_step, 0, unroll=side)
            if not last:
                for off, peer in peers:
                    sum_copy(sweep, part_no, off, peer, me).start()
                sums[sweep, me, part_no] = part[sweep, part_no]
            else:
                for c in range(CHUNKS):
                    tally(part_no, c)

    for off, peer in peers:
        end_copy(off, peer, me).start()
    end_sums[me] = end_part[me]

    first_year = b * GROUP
    g = [gain[pl.ds(first_year + i, 1), :] for i in range(GROUP)]
    r = [back[pl.ds(first_year + i, 1), :] for i in range(GROUP)]
    w = [share[pl.ds(first_year + i, 1), :] for i in range(GROUP)]
    keep = []
    for i in range(GROUP):
        keep.append((1.0 - g[i]) * keep[-1] if i else 1.0 - g[i])
    hold = [jnp.ones_like(g[0])]
    for i in reversed(range(GROUP)):
        hold.insert(0, (1.0 - r[i]) * hold[0])
    block_keep, block_hold = [], []
    for other in range(n_blocks):
        years = range(other * GROUP, (other + 1) * GROUP)
        block_keep.append(functools.reduce(jnp.multiply, [1.0 - gain[y : y + 1, :] for y in years]))
        block_hold.append(functools.reduce(jnp.multiply, [1.0 - back[y : y + 1, :] for y in years]))
    into = []
    for other in range(n_blocks):
        fore = jnp.where(other < b, 1.0, 0.0)
        for between in range(other + 1, n_blocks):
            fore = fore * jnp.where(between < b, block_keep[between], 1.0)
        hind = jnp.where(other > b, 1.0, 0.0)
        for between in range(other):
            hind = hind * jnp.where(between > b, block_hold[between], 1.0)
        into.append((fore, hind))

    def mid_copy(c, off, other, source):
        which = jnp.where(other > b, 0, 1)
        return send(mid_out.at[c, which], mid_in.at[c, source], mid_send.at[c, off], mid_recv.at[c, source], other_id(off, other))

    for off, peer in peers:
        msg_copy(off, peer, me).wait_send()
        for sweep in range(EITERS - 1):
            for part_no in range(parts):
                sum_copy(sweep, part_no, off, peer, me).wait_send()

    for c in range(CHUNKS):
        years_in[c, m] = pseudo[word_rows(m, c), :]
        mid_in[c, b] = jnp.zeros((width, K), jnp.int16)
        for off, mate in mates:
            in_copy(c, mate, mate).wait_recv()
        values = [decode(years_in[c, i]) for i in range(GROUP)]
        ahead = g[0] * values[0]
        local[c, 0] = w[0] * ahead
        for i in range(1, GROUP):
            ahead = g[i] * values[i] + (1.0 - g[i]) * ahead
            local[c, i] = w[i] * ahead
        mid_out[c, 0] = encode(ahead)
        behind = r[GROUP - 1] * values[GROUP - 1]
        for i in reversed(range(GROUP - 1)):
            local[c, i] += (1.0 - w[i]) * behind
            behind = r[i] * values[i] + (1.0 - r[i]) * behind
        mid_out[c, 1] = encode(behind)
        for off, other in others:
            mid_copy(c, off, other, b).start()

    def out_copy(c, mate, source):
        return send(
            years_out.at[c, mate], coded.at[word_rows(source, c), :], out_send.at[c, mate], out_recv.at[c, source], mate_id(mate)
        )

    for c in range(CHUNKS):
        for off, other in others:
            mid_copy(c, off, other, other).wait_recv()
        ahead, behind = 0.0, 0.0
        for other in range(n_blocks):
            value = decode(mid_in[c, other])
            ahead = ahead + into[other][0] * value
            behind = behind + into[other][1] * value
        for i in range(GROUP):
            years_out[c, i] = encode(local[c, i] + (w[i] * keep[i]) * ahead + ((1.0 - w[i]) * hold[i + 1]) * behind)
        for off, mate in mates:
            out_copy(c, mate, m).start()
        out_ref[word_rows(m, c), :] = decode(years_out[c, m])

    for off, peer in peers:
        end_copy(off, peer, peer).wait_recv()
    whole = end_sums[0]
    for s in range(1, n_doc):
        whole = whole + end_sums[s]
    topics_ref[...] = prior + whole

    for off, peer in peers:
        end_copy(off, peer, me).wait_send()
    for c in range(CHUNKS):
        for off, mate in mates:
            in_copy(c, mate, m).wait_send()
    for c in range(CHUNKS):
        for off, other in others:
            mid_copy(c, off, other, b).wait_send()
    for c in range(CHUNKS):
        for off, mate in mates:
            out_copy(c, mate, mate).wait_recv()
            out_ref[word_rows(mate, c), :] = decode(coded[word_rows(mate, c), :])
    for c in range(CHUNKS):
        for off, mate in mates:
            out_copy(c, mate, m).wait_send()


def vmem():
    return pl.BlockSpec(memory_space=pltpu.VMEM)


def solution(mesh):
    n_tm, n_doc = mesh.shape["tm"], mesh.shape["doc"]

    def body(beta, word_ids, word_counts, block_slot, topic_prior, drift_var, obs_precision):
        local_beta, ids, cnt = beta[0], word_ids[0], word_counts[0]
        own, dpd = local_beta.shape[0], ids.shape[0]
        held = dpd * 128
        width = own // GROUP // CHUNKS
        n_blocks = n_tm // GROUP
        parts = min(PARTS, n_doc)
        lot = n_doc // parts * dpd
        f32, bf16, link = jnp.float32, jnp.bfloat16, jnp.int16
        dma = pltpu.SemaphoreType.DMA
        smoothed, doc_topics = pl.pallas_call(
            functools.partial(kernel, n_tm, n_doc),
            out_shape=(jax.ShapeDtypeStruct((own, K), f32), jax.ShapeDtypeStruct((dpd, K), f32)),
            in_specs=[pl.BlockSpec(memory_space=pltpu.HBM)] * 7,
            out_specs=(vmem(), vmem()),
            scratch_shapes=[
                pltpu.VMEM((own, K), f32),
                pltpu.VMEM((dpd, 128), jnp.int32),
                pltpu.VMEM((dpd, 128), jnp.int32),
                pltpu.SMEM(block_slot.shape, jnp.int32),
                pltpu.VMEM((1, K), f32),
                pltpu.VMEM((n_tm, K), f32),
                pltpu.VMEM((1, K), f32),
                dma((7,)),
                pltpu.VMEM((16, K), f32),
                pltpu.VMEM((n_doc, 16, K), f32),
                pltpu.VMEM((own // FOLD, FOLD * K), bf16),
                pltpu.VMEM((n_doc * held, K), f32),
                pltpu.VMEM((n_doc * held, K), f32),
                pltpu.VMEM((n_doc * held, K), f32),
                pltpu.VMEM((n_doc * held, FOLD * K), bf16),
                pltpu.VMEM((CHUNKS, own // FOLD // CHUNKS, FOLD * K), f32),
                pltpu.VMEM((parts, lot, K), f32),
                pltpu.VMEM((EITERS - 1, parts, lot, K), f32),
                pltpu.VMEM((EITERS - 1, n_doc, parts, lot, K), f32),
                pltpu.VMEM((n_doc, dpd, K), f32),
                pltpu.VMEM((n_doc, dpd, K), f32),
                pltpu.VMEM((n_tm, K), f32),
                pltpu.VMEM((n_tm, K), f32),
                pltpu.VMEM((n_tm, K), f32),
                pltpu.VMEM((own, K), link),
                pltpu.VMEM((CHUNKS, GROUP, width, K), link),
                pltpu.VMEM((CHUNKS, GROUP, width, K), f32),
                pltpu.VMEM((CHUNKS, 2, width, K), link),
                pltpu.VMEM((CHUNKS, n_blocks, width, K), link),
                pltpu.VMEM((CHUNKS, GROUP, width, K), link),
                pltpu.VMEM((own, K), link),
                dma((n_doc,)),
                dma((n_doc,)),
                dma((parts * (EITERS - 1), n_doc)),
                dma((parts * (EITERS - 1), n_doc)),
                dma((n_doc,)),
                dma((n_doc,)),
                dma((CHUNKS, GROUP)),
                dma((CHUNKS, GROUP)),
                dma((CHUNKS, n_blocks)),
                dma((CHUNKS, n_blocks)),
                dma((CHUNKS, GROUP)),
                dma((CHUNKS, GROUP)),
            ],
            compiler_params=pltpu.CompilerParams(
                collective_id=0, has_side_effects=True, vmem_limit_bytes=48 * 1024 * 1024
            ),
            name="topics",
        )(*[
            pltpu.with_memory_space_constraint(a, pltpu.HBM)
            for a in (local_beta, ids, cnt, block_slot, topic_prior[None], obs_precision, drift_var[None])
        ])
        return (smoothed[None], doc_topics[None])

    in_specs = (P("tm", "doc", None), P("tm", "doc", None), P("tm", "doc", None), P(), P(), P(), P())
    out_specs = (P("tm", "doc", None), P("tm", "doc", None))
    return jax.shard_map(body, mesh=mesh, in_specs=in_specs, out_specs=out_specs, check_vma=False)
```
